32 devices in a mesh: grp: 2 (over y), own: 16 (over z, x, core).
Axes of the slice: x: 2, y: 2, z: 4, core: 2. Of those that a mesh axis runs over, the one named last changes fastest.
Arguments:
- amplitudes: bfloat16 [192, 32, 128], P('own', 'grp'), may hold values from -6 to 6
- integrals: bfloat16 [12288, 2048], P('own', 'grp'), may hold values from -0.109375 to 0.109375
- tile_block: int32 [192], P('own'), may hold values from 0 to 7, as said below
- tile_index: int32 [192], P('own'), may hold values from 0 to 95, as said below
Outputs:
- ladder: float32 [256, 2048], P('own', 'grp')
The draws below stay inside these ranges and needn't reach their ends.
Inputs may be any that keep to these rules, and one draw needn't show every extreme that they name: Each pair (tile_block, tile_index) is named by at most one of the 192 tile rows. Of the 12 rows of one own index, at most 2 have tile_index in one owner's range o * 6 to (o + 1) * 6 - 1, and exactly 2 do for some owners. Exactly 12 of all tile rows have tile_index in each owner's range. `tile_index`: owner o holds integral rows of tiles o * 6 to (o + 1) * 6 - 1.
All inputs are finite; a program needn't handle non-finite values.
Results may differ from the reference program's by a relative error of at most 0.0003.
Values may be sent and summed in bfloat16 or wider, within the bound.
A program may use at most 64 MiB of HBM per device.

```python
import jax
import jax.numpy as jnp
from jax import lax

TS = 128
TILE_DEV = 6
NB = 8
OCC = 32
ROWS_DEV = 12
ROWS = 192
CD = 12288
AB = 2048


def tile_plan(key):
    source_count = ROWS // ROWS_DEV
    keys_owner = NB * TILE_DEV
    eighth = source_count // 8
    key_pattern, key_rotate, key_owner, key_shuffle = jax.random.split(jax.random.fold_in(key, 7), 4)
    owner_pos = jnp.arange(source_count)
    pattern = jnp.where(owner_pos < 2 * eighth, 2, jnp.where(owner_pos < 4 * eighth, 1, 0)).astype(jnp.int32)
    pattern = jax.random.permutation(key_pattern, pattern)
    rotation = jax.random.permutation(key_rotate, source_count).astype(jnp.int32)
    counts = pattern[(owner_pos[None, :] - rotation[:, None]) % source_count]
    offsets = jnp.cumsum(counts, axis=0) - counts
    owner_perm = jax.vmap(lambda k: jax.random.permutation(k, keys_owner))(jax.random.split(key_owner, source_count)).astype(jnp.int32)

    def one_source(c, o, k):
        cum_ends = jnp.cumsum(c)
        j = jnp.arange(ROWS_DEV)
        row_owner = jnp.searchsorted(cum_ends, j, side='right').astype(jnp.int32)
        within_rank = j - (cum_ends[row_owner] - c[row_owner])
        key_slot = o[row_owner] + within_rank
        key_values = owner_perm[row_owner, key_slot]
        shuffle = jax.random.permutation(k, ROWS_DEV)
        return (row_owner[shuffle], key_values[shuffle])
    owners, key_values = jax.vmap(one_source)(counts, offsets, jax.random.split(key_shuffle, source_count))
    row_block = (key_values // TILE_DEV).astype(jnp.int32)
    row_tile = (owners * TILE_DEV + key_values % TILE_DEV).astype(jnp.int32)
    return (row_block.reshape(-1), row_tile.reshape(-1))


def draw_tile_block(key, part):
    return tile_plan(key)[0]


def draw_tile_index(key, part):
    return tile_plan(key)[1]


def levels(key, dims, shards, smallest, top_value):
    def one(axis_at, shards_of):
        steps = jax.random.uniform(jax.random.fold_in(jax.random.fold_in(key, 6), axis_at), (shards_of,), jnp.float32, smallest / len(shards), top_value / len(shards))
        return jnp.repeat(jnp.exp(steps), dims[axis_at] // shards_of).reshape((-1,) + (1,) * (len(dims) - axis_at - 1))

    factor_of = one(*shards[0])
    for cut in shards[1:]:
        factor_of = factor_of * one(*cut)
    return factor_of


def gaussian(rng, dims, deviation, most, cuts=(), dtype=jnp.bfloat16):
    gain = levels(rng, dims, cuts, -0.22, 0.18) if cuts else 1.0
    drawn = jax.random.normal(rng, dims, jnp.float32) * deviation * gain
    return jnp.minimum(jnp.maximum(drawn, -most), most).astype(dtype)


def setup_inputs(seed: int = 0) -> dict:
    streams_of = jax.random.split(jax.random.key(seed), 5)
    return {
        "amplitudes": gaussian(streams_of[0], (ROWS, OCC, TS), 1.0, 6.0, ((0, 16), (1, 2))),
        "integrals": gaussian(streams_of[1], (CD, AB), (ROWS * TS // NB) ** -0.5, 0.109375, ((0, 16), (1, 2))),
        "tile_block": draw_tile_block(jax.random.fold_in(streams_of[4], 71), 0),
        "tile_index": draw_tile_index(jax.random.fold_in(streams_of[4], 71), 0),
    }


def reference(amplitudes, integrals, tile_block, tile_index):
    occ_rows = amplitudes.shape[1]
    tile_width = amplitudes.shape[2]
    totals = jnp.zeros((NB * occ_rows, integrals.shape[1]), jnp.float32)

    def add_tile(running, scanned):
        amp_tile, row_block, row_tile = scanned
        columns = lax.dynamic_slice_in_dim(integrals, (row_tile * tile_width).astype(jnp.int32), tile_width, 0)
        product = jnp.dot(amp_tile, columns, preferred_element_type=jnp.float32)
        row_start = (row_block * occ_rows).astype(jnp.int32)
        current = lax.dynamic_slice_in_dim(running, row_start, occ_rows, 0)
        return lax.dynamic_update_slice_in_dim(running, current + product, row_start, 0), None

    ladder, _ = lax.scan(add_tile, totals, (amplitudes, tile_block, tile_index))
    return ladder
```

```python
import functools

import jax
import jax.numpy as jnp
from jax import lax
from jax.experimental import pallas as pl
from jax.experimental.pallas import tpu as pltpu
from jax.sharding import PartitionSpec as P

NB = 8
CAP = 2
MESH = pl.DeviceIdType.MESH
ORDER = (8, 7, 9, 6, 10, 5, 11, 4, 12, 3, 13, 2, 14, 1, 15)
ZORDER = (2, 1, 3, 0)


def local(amplitudes, integrals, tile_block, tile_index):
    own_count = lax.axis_size("own")
    tile_width = amplitudes.shape[2]
    tile_dev = integrals.shape[0] // tile_width
    tile_owner = tile_index // tile_dev
    local_tile = tile_index - tile_owner * tile_dev
    tile_key = tile_block * tile_dev + local_tile
    one_hot = (tile_owner[:, None] == jnp.arange(own_count)[None, :]).astype(jnp.int32)
    slot_rank = jnp.sum((jnp.cumsum(one_hot, axis=0) - one_hot) * one_hot, axis=1)
    key_buffer = jnp.full((own_count, CAP), -1, jnp.int32).at[tile_owner, slot_rank].set(tile_key)
    gathered = lax.all_gather(amplitudes, "grp", axis=1, tiled=True)
    buffer = jnp.zeros((own_count, CAP) + gathered.shape[1:], gathered.dtype)
    received = lax.all_to_all(
        buffer.at[tile_owner, slot_rank].set(gathered),
        "own",
        split_axis=0,
        concat_axis=0,
        tiled=True,
    )
    recv_keys = lax.all_to_all(key_buffer, "own", split_axis=0, concat_axis=0, tiled=True)
    occ_rows = received.shape[2]
    slots = received.reshape(own_count * CAP, occ_rows, tile_width)
    flat_keys = recv_keys.reshape(own_count * CAP)
    recv_block = jnp.where(flat_keys >= 0, flat_keys // tile_dev, -1)
    recv_tile = jnp.where(flat_keys >= 0, flat_keys % tile_dev, 0)
    row_count = NB * occ_rows
    row_index = recv_block[:, None] * occ_rows + jnp.arange(occ_rows)[None, :]
    in_range = (recv_block[:, None] >= 0) & (row_index >= 0) & (row_index < row_count)
    row_index = jnp.where(in_range, row_index, row_count)
    tile_slot = jnp.broadcast_to(recv_tile[:, None], row_index.shape)
    placed = jnp.zeros((row_count, tile_dev, tile_width), slots.dtype)
    placed = placed.at[row_index, tile_slot].set(slots, mode="drop")
    return lax.psum_scatter(
        jnp.dot(
            placed.reshape(row_count, tile_dev * tile_width),
            integrals,
            preferred_element_type=jnp.float32,
        ),
        "own",
        scatter_dimension=0,
        tiled=True,
    )


def encode(v):
    parts = [v[:, k * 128 : (k + 1) * 128] for k in range(8)]
    top = functools.reduce(jnp.maximum, [jnp.abs(p) for p in parts])
    expo = jnp.ceil(jnp.log2(jnp.maximum(top, 1e-30)))
    scale = jnp.exp2(15.0 - expo)
    coded = [jnp.clip(jnp.round(p * scale), -32767.0, 32767.0) for p in parts] + [expo]
    return jnp.concatenate(coded, axis=1).astype(jnp.int32).astype(jnp.int16)


def decode(q):
    wide = q.astype(jnp.int32).astype(jnp.float32)
    scale = jnp.exp2(wide[:, 1024:] - 15.0)
    return jnp.concatenate([wide[:, k * 128 : (k + 1) * 128] * scale for k in range(8)], axis=1)


def kernel(
    block_ref, index_ref, amp_ref, int_hbm, out_ref,
    ints, sends, recvs, others, key_out, key_in, pick, lhs, prod, sib,
    x_out, x_in, z_out, z_in,
    int_sem, tile_ss, tile_rs, key_ss, key_rs, fwd_ss, fwd_rs,
    core_ss, core_rs, x_ss, x_rs, z_ss, z_rs,
):
    n = 16
    rows = amp_ref.shape[0] // 16
    tile_dev = 6
    me = lax.axis_index("own")
    g = lax.axis_index("grp")
    core = lax.rem(me, 2)
    x = lax.rem(me // 2, 2)
    z = me // 4
    sibling = me + 1 - 2 * core
    across = me + 2 - 4 * x

    load = pltpu.make_async_copy(int_hbm, ints, int_sem)
    load.start()
    barrier = pltpu.get_barrier_semaphore()
    for d in range(1, n):
        pl.semaphore_signal(barrier, inc=1, device_id={"own": lax.rem(me + d, n)}, device_id_type=MESH)
    pl.semaphore_signal(barrier, inc=1, device_id={"grp": 1 - g}, device_id_type=MESH)

    owner, rank, key = [], [], []
    for r in range(rows):
        t = index_ref[r]
        o = t // tile_dev
        owner.append(o)
        key.append((t - o * tile_dev) * NB + block_ref[r])
        earlier = jnp.int32(0)
        for q in range(r):
            earlier = earlier + jnp.where(owner[q] == o, 1, 0)
        rank.append(earlier)

    dest = lax.broadcasted_iota(jnp.int32, (n, 128), 0)
    lane = lax.broadcasted_iota(jnp.int32, (n, 128), 1)
    sub = lane - lax.rem(me, 4) * 32
    slot = jnp.where((sub >= 0) & (sub < 32), dest * 2 + sub // 16, -1)
    inner = lax.rem(lane, 16)
    keys = jnp.zeros((n, 128), jnp.int32)
    for r in range(rows):
        keys = keys + jnp.where(slot == owner[r] * 2 + rank[r], key[r] * 16 + inner + 1, 0)
    for o in range(n):
        key_out[o] = keys[o : o + 1, :]

    col = lax.broadcasted_iota(jnp.int32, (1, rows * 16), 1)
    place = jnp.zeros((1, rows * 16), jnp.int32)
    for r in range(rows):
        place = jnp.where(col // 16 == r, (owner[r] * 2 + rank[r]) * 16 + lax.rem(col, 16), place)
    amp = amp_ref[...]
    for part in range(4):
        row = lax.broadcasted_iota(jnp.int32, (128, rows * 16), 0) + part * 128
        hot = jnp.where(row == place, 1.0, 0.0).astype(jnp.bfloat16)
        got = jnp.dot(hot, amp, preferred_element_type=jnp.float32).astype(jnp.bfloat16)
        sends[pl.ds(part * 4, 4)] = got.reshape(4, 32, 128)
    recvs[me] = sends[me]
    key_in[me] = key_out[me]

    pl.semaphore_wait(barrier, n)

    def key_copy(to):
        return pltpu.make_async_remote_copy(
            key_out.at[to], key_in.at[me], key_ss.at[to], key_rs.at[me],
            device_id={"own": to}, device_id_type=MESH,
        )

    def tile_copy(to):
        return pltpu.make_async_remote_copy(
            sends.at[to], recvs.at[me], tile_ss.at[to], tile_rs.at[me],
            device_id={"own": to}, device_id_type=MESH,
        )

    def forward(s):
        return pltpu.make_async_remote_copy(
            recvs.at[s], others.at[s], fwd_ss.at[s], fwd_rs.at[s],
            device_id={"grp": 1 - g}, device_id_type=MESH,
        )

    for d in ORDER:
        key_copy(lax.rem(me + d, n)).start()
    for d in ORDER:
        tile_copy(lax.rem(me + d, n)).start()
    forward(me).start()

    def arrived(s, buffer, sem):
        return pltpu.make_async_remote_copy(
            buffer.at[s], buffer.at[s], sem.at[s], sem.at[s],
            device_id={"own": sibling}, device_id_type=MESH,
        )

    for d in ORDER:
        arrived(lax.rem(me + n - d, n), key_in, key_rs).wait_recv()
    targets = [
        key_in[4 * j] + key_in[4 * j + 1] + key_in[4 * j + 2] + key_in[4 * j + 3] for j in range(4)
    ]
    target = jnp.concatenate(targets, axis=1)
    for t in range(tile_dev):
        row = lax.broadcasted_iota(jnp.int32, (128, 512), 0) + (t * 128 + 1)
        pick[t] = jnp.where(row == target, 1.0, 0.0).astype(jnp.bfloat16)

    for d in reversed(ORDER):
        s = lax.rem(me + n - d, n)
        arrived(s, recvs, tile_rs).wait_recv()
        forward(s).start()

    def half(h, source):
        tiles = source[...].reshape(512, 128)
        for t in range(tile_dev):
            lhs[:, t * 128 : (t + 1) * 128] = jnp.dot(
                pick[t], tiles, preferred_element_type=jnp.float32
            ).astype(jnp.bfloat16)
        if h == 0:
            load.wait()
        for k in range(4):
            prod[h, k] = jnp.dot(
                lhs[...], ints[:, k * 256 : (k + 1) * 256], preferred_element_type=jnp.float32
            ).reshape(8, 16, 256)

    def core_copy(h, k):
        return pltpu.make_async_remote_copy(
            prod.at[h, k], sib.at[k], core_ss.at[k], core_rs.at[k],
            device_id={"own": sibling}, device_id_type=MESH,
        )

    mine_first = core == g

    half(0, recvs)

    @pl.when(jnp.logical_not(mine_first))
    def _():
        for k in range(4):
            core_copy(0, k).start()

    for d in range(n):
        arrived(lax.rem(me + d, n), others, fwd_rs).wait_recv()
    half(1, others)

    @pl.when(mine_first)
    def _():
        for k in range(4):
            core_copy(1, k).start()

    for k in range(4):
        core_copy(0, k).wait_recv()
    keep = lax.rem(core + g, 2)

    def chip_sum(b):
        return jnp.concatenate([prod[keep, k, b] + sib[k, b] for k in range(4)], axis=1)

    def x_copy(dz):
        return pltpu.make_async_remote_copy(
            x_out.at[dz], x_in.at[dz], x_ss.at[dz], x_rs.at[dz],
            device_id={"own": across}, device_id_type=MESH,
        )

    def z_copy(dz):
        return pltpu.make_async_remote_copy(
            z_out.at[dz], z_in.at[dz], z_ss.at[dz], z_rs.at[dz],
            device_id={"own": lax.rem(me + 4 * dz, n)}, device_id_type=MESH,
        )

    for dz in ZORDER:
        to_z = lax.rem(z + dz, 4)
        x_out[dz] = encode(chip_sum(to_z * 2 + 1 - x))
        x_copy(dz).start()
    for dz in ZORDER:
        to_z = lax.rem(z + dz, 4)
        total = chip_sum(to_z * 2 + x)
        x_copy(dz).wait_recv()
        total = total + decode(x_in[dz])
        if dz:
            z_out[dz] = encode(total)
            z_copy(dz).start()
        else:
            out_ref[...] = total
    for dz in (1, 3, 2):
        z_copy(dz).wait_recv()
        out_ref[...] += decode(z_in[dz])

    for d in ORDER:
        to = lax.rem(me + d, n)
        key_copy(to).wait_send()
        tile_copy(to).wait_send()
    for s in range(n):
        forward(s).wait_send()
    for k in range(4):
        core_copy(0, k).wait_send()
    for dz in range(4):
        x_copy(dz).wait_send()
        if dz:
            z_copy(dz).wait_send()


def fused(amplitudes, integrals, tile_block, tile_index):
    rows = amplitudes.shape[0]
    dma = pltpu.SemaphoreType.DMA
    bf16, f32, i32, i16 = jnp.bfloat16, jnp.float32, jnp.int32, jnp.int16
    return pl.pallas_call(
        kernel,
        out_shape=jax.ShapeDtypeStruct((16, 1024), f32),
        in_specs=[
            pl.BlockSpec(memory_space=pltpu.SMEM),
            pl.BlockSpec(memory_space=pltpu.SMEM),
            pl.BlockSpec(memory_space=pltpu.VMEM),
            pl.BlockSpec(memory_space=pl.ANY),
        ],
        out_specs=pl.BlockSpec(memory_space=pltpu.VMEM),
        scratch_shapes=[
            pltpu.VMEM((768, 1024), bf16),
            pltpu.VMEM((16, 32, 128), bf16),
            pltpu.VMEM((16, 32, 128), bf16),
            pltpu.VMEM((16, 32, 128), bf16),
            pltpu.VMEM((16, 1, 128), i32),
            pltpu.VMEM((16, 1, 128), i32),
            pltpu.VMEM((6, 128, 512), bf16),
            pltpu.VMEM((128, 768), bf16),
            pltpu.VMEM((2, 4, 8, 16, 256), f32),
            pltpu.VMEM((4, 8, 16, 256), f32),
            pltpu.VMEM((4, 16, 1152), i16),
            pltpu.VMEM((4, 16, 1152), i16),
            pltpu.VMEM((4, 16, 1152), i16),
            pltpu.VMEM((4, 16, 1152), i16),
            dma(()), dma((16,)), dma((16,)), dma((16,)), dma((16,)), dma((16,)), dma((16,)),
            dma((4,)), dma((4,)), dma((4,)), dma((4,)), dma((4,)), dma((4,)),
        ],
        compiler_params=pltpu.CompilerParams(
            collective_id=0, has_side_effects=True, vmem_limit_bytes=24 * 1024 * 1024
        ),
        name="ladder",
    )(tile_block, tile_index, amplitudes.reshape(rows * 16, 128), integrals)


def solution(mesh):
    count = (mesh.shape["grp"], mesh.shape["own"])

    def run(amplitudes, integrals, tile_block, tile_index):
        sizes = amplitudes.shape + integrals.shape
        small = count == (2, 16) and sizes == (192, 32, 128, 12288, 2048)
        return jax.shard_map(
            fused if small else local,
            mesh=mesh,
            in_specs=(P("own", "grp", None), P("own", "grp"), P("own"), P("own")),
            out_specs=P("own", "grp"),
            check_vma=False,
        )(amplitudes, integrals, tile_block, tile_index)

    return run
```

```python
import functools

import jax
import jax.numpy as jnp
from jax import lax
from jax.experimental import pallas as pl
from jax.experimental.pallas import tpu as pltpu
from jax.sharding import PartitionSpec as P

NB = 8
CAP = 2
MESH = pl.DeviceIdType.MESH
ORDER = (8, 7, 9, 6, 10, 5, 11, 4, 12, 3, 13, 2, 14, 1, 15)
ZORDER = (2, 1, 3, 0)


def local(amplitudes, integrals, tile_block, tile_index):
    own_count = lax.axis_size("own")
    tile_width = amplitudes.shape[2]
    tile_dev = integrals.shape[0] // tile_width
    tile_owner = tile_index // tile_dev
    local_tile = tile_index - tile_owner * tile_dev
    tile_key = tile_block * tile_dev + local_tile
    one_hot = (tile_owner[:, None] == jnp.arange(own_count)[None, :]).astype(jnp.int32)
    slot_rank = jnp.sum((jnp.cumsum(one_hot, axis=0) - one_hot) * one_hot, axis=1)
    key_buffer = jnp.full((own_count, CAP), -1, jnp.int32).at[tile_owner, slot_rank].set(tile_key)
    gathered = lax.all_gather(amplitudes, "grp", axis=1, tiled=True)
    buffer = jnp.zeros((own_count, CAP) + gathered.shape[1:], gathered.dtype)
    received = lax.all_to_all(
        buffer.at[tile_owner, slot_rank].set(gathered),
        "own",
        split_axis=0,
        concat_axis=0,
        tiled=True,
    )
    recv_keys = lax.all_to_all(key_buffer, "own", split_axis=0, concat_axis=0, tiled=True)
    occ_rows = received.shape[2]
    slots = received.reshape(own_count * CAP, occ_rows, tile_width)
    flat_keys = recv_keys.reshape(own_count * CAP)
    recv_block = jnp.where(flat_keys >= 0, flat_keys // tile_dev, -1)
    recv_tile = jnp.where(flat_keys >= 0, flat_keys % tile_dev, 0)
    row_count = NB * occ_rows
    row_index = recv_block[:, None] * occ_rows + jnp.arange(occ_rows)[None, :]
    in_range = (recv_block[:, None] >= 0) & (row_index >= 0) & (row_index < row_count)
    row_index = jnp.where(in_range, row_index, row_count)
    tile_slot = jnp.broadcast_to(recv_tile[:, None], row_index.shape)
    placed = jnp.zeros((row_count, tile_dev, tile_width), slots.dtype)
    placed = placed.at[row_index, tile_slot].set(slots, mode="drop")
    return lax.psum_scatter(
        jnp.dot(
            placed.reshape(row_count, tile_dev * tile_width),
            integrals,
            preferred_element_type=jnp.float32,
        ),
        "own",
        scatter_dimension=0,
        tiled=True,
    )


def encode(v):
    parts = [v[:, k * 128 : (k + 1) * 128] for k in range(8)]
    top = functools.reduce(jnp.maximum, [jnp.abs(p) for p in parts])
    expo = jnp.ceil(jnp.log2(jnp.maximum(top, 1e-30)))
    scale = jnp.exp2(15.0 - expo)
    coded = [jnp.clip(jnp.round(p * scale), -32767.0, 32767.0) for p in parts] + [expo]
    return jnp.concatenate(coded, axis=1).astype(jnp.int32).astype(jnp.int16)


def decode(q):
    wide = q.astype(jnp.int32).astype(jnp.float32)
    scale = jnp.exp2(wide[:, 1024:] - 15.0)
    return jnp.concatenate([wide[:, k * 128 : (k + 1) * 128] * scale for k in range(8)], axis=1)


def kernel(
    block_hbm, index_hbm, amp_hbm, int_hbm, out_ref,
    block_ref, index_ref, amp_ref, ints, sends, recvs, others, key_out, key_in, pick, lhs, prod, sib,
    x_out, x_in, z_out, z_in,
    int_sem, amp_sem, block_sem, index_sem, tile_ss, tile_rs, key_ss, key_rs, fwd_ss, fwd_rs,
    core_ss, core_rs, x_ss, x_rs, z_ss, z_rs,
):
    n = 16
    rows = amp_ref.shape[0] // 16
    tile_dev = 6
    me = lax.axis_index("own")
    g = lax.axis_index("grp")
    core = lax.rem(me, 2)
    x = lax.rem(me // 2, 2)
    z = me // 4
    sibling = me + 1 - 2 * core
    across = me + 2 - 4 * x

    load_index = pltpu.make_async_copy(index_hbm, index_ref, index_sem)
    load_block = pltpu.make_async_copy(block_hbm, block_ref, block_sem)
    load_amp = pltpu.make_async_copy(amp_hbm, amp_ref, amp_sem)
    load = pltpu.make_async_copy(int_hbm, ints, int_sem)
    load_index.start()
    load_block.start()
    load_amp.start()
    barrier = pltpu.get_barrier_semaphore()
    for d in range(1, n):
        pl.semaphore_signal(barrier, inc=1, device_id={"own": lax.rem(me + d, n)}, device_id_type=MESH)
    pl.semaphore_signal(barrier, inc=1, device_id={"grp": 1 - g}, device_id_type=MESH)

    load.start()
    load_index.wait()
    load_block.wait()

    owner, rank, key = [], [], []
    for r in range(rows):
        t = index_ref[r]
        o = t // tile_dev
        owner.append(o)
        key.append((t - o * tile_dev) * NB + block_ref[r])
        earlier = jnp.int32(0)
        for q in range(r):
            earlier = earlier + jnp.where(owner[q] == o, 1, 0)
        rank.append(earlier)

    dest = lax.broadcasted_iota(jnp.int32, (n, 128), 0)
    lane = lax.broadcasted_iota(jnp.int32, (n, 128), 1)
    sub = lane - lax.rem(me, 4) * 32
    slot = jnp.where((sub >= 0) & (sub < 32), dest * 2 + sub // 16, -1)
    inner = lax.rem(lane, 16)
    keys = jnp.zeros((n, 128), jnp.int32)
    for r in range(rows):
        keys = keys + jnp.where(slot == owner[r] * 2 + rank[r], key[r] * 16 + inner + 1, 0)
    for o in range(n):
        key_out[o] = keys[o : o + 1, :]

    col = lax.broadcasted_iota(jnp.int32, (1, rows * 16), 1)
    place = jnp.zeros((1, rows * 16), jnp.int32)
    for r in range(rows):
        place = jnp.where(col // 16 == r, (owner[r] * 2 + rank[r]) * 16 + lax.rem(col, 16), place)
    load_amp.wait()
    amp = amp_ref[...]
    for part in range(4):
        row = lax.broadcasted_iota(jnp.int32, (128, rows * 16), 0) + part * 128
        hot = jnp.where(row == place, 1.0, 0.0).astype(jnp.bfloat16)
        got = jnp.dot(hot, amp, preferred_element_type=jnp.float32).astype(jnp.bfloat16)
        sends[pl.ds(part * 4, 4)] = got.reshape(4, 32, 128)
    recvs[me] = sends[me]
    key_in[me] = key_out[me]

    pl.semaphore_wait(barrier, n)

    def key_copy(to):
        return pltpu.make_async_remote_copy(
            key_out.at[to], key_in.at[me], key_ss.at[to], key_rs.at[me],
            device_id={"own": to}, device_id_type=MESH,
        )

    def tile_copy(to):
        return pltpu.make_async_remote_copy(
            sends.at[to], recvs.at[me], tile_ss.at[to], tile_rs.at[me],
            device_id={"own": to}, device_id_type=MESH,
        )

    def forward(j):
        return pltpu.make_async_remote_copy(
            recvs.at[pl.ds(j * 4, 4)], others.at[pl.ds(j * 4, 4)], fwd_ss.at[j], fwd_rs.at[j],
            device_id={"grp": 1 - g}, device_id_type=MESH,
        )

    for d in ORDER:
        key_copy(lax.rem(me + d, n)).start()
    for d in ORDER:
        tile_copy(lax.rem(me + d, n)).start()

    def arrived(s, buffer, sem):
        return pltpu.make_async_remote_copy(
            buffer.at[s], buffer.at[s], sem.at[s], sem.at[s],
            device_id={"own": sibling}, device_id_type=MESH,
        )

    for d in ORDER:
        arrived(lax.rem(me + n - d, n), key_in, key_rs).wait_recv()
    targets = [
        key_in[4 * j] + key_in[4 * j + 1] + key_in[4 * j + 2] + key_in[4 * j + 3] for j in range(4)
    ]
    target = jnp.concatenate(targets, axis=1)
    for t in range(tile_dev):
        row = lax.broadcasted_iota(jnp.int32, (128, 512), 0) + (t * 128 + 1)
        pick[t * 128 : (t + 1) * 128, :] = jnp.where(row == target, 1.0, 0.0).astype(jnp.bfloat16)

    for dz in (0, 1, 3, 2):
        j = lax.rem(z + dz, 4)
        for w in range(4):
            if dz or w:
                arrived(j * 4 + lax.rem(me + w, 4), recvs, tile_rs).wait_recv()
        forward(j).start()

    mine_first = core == g

    def half(h, source):
        tiles = source[...].reshape(512, 128)
        got = jnp.dot(pick[...], tiles, preferred_element_type=jnp.float32).astype(jnp.bfloat16)
        for t in range(tile_dev):
            lhs[:, t * 128 : (t + 1) * 128] = got[t * 128 : (t + 1) * 128]
        if h == 0:
            load.wait()
        for k in range(4):
            prod[h, k] = jnp.dot(
                lhs[...], ints[:, k * 256 : (k + 1) * 256], preferred_element_type=jnp.float32
            ).reshape(8, 16, 256)

            @pl.when(mine_first == (h == 1))
            def _():
                core_copy(h, k).start()

    def core_copy(h, k):
        return pltpu.make_async_remote_copy(
            prod.at[h, k], sib.at[k], core_ss.at[k], core_rs.at[k],
            device_id={"own": sibling}, device_id_type=MESH,
        )

    half(0, recvs)
    for j in range(4):
        forward(j).wait_recv()
    half(1, others)

    for k in range(4):
        core_copy(0, k).wait_recv()
    keep = lax.rem(core + g, 2)

    def chip_sum(b):
        return jnp.concatenate([prod[keep, k, b] + sib[k, b] for k in range(4)], axis=1)

    def x_copy(dz):
        return pltpu.make_async_remote_copy(
            x_out.at[dz], x_in.at[dz], x_ss.at[dz], x_rs.at[dz],
            device_id={"own": across}, device_id_type=MESH,
        )

    def z_copy(dz):
        return pltpu.make_async_remote_copy(
            z_out.at[dz], z_in.at[dz], z_ss.at[dz], z_rs.at[dz],
            device_id={"own": lax.rem(me + 4 * dz, n)}, device_id_type=MESH,
        )

    for dz in ZORDER:
        to_z = lax.rem(z + dz, 4)
        x_out[dz] = encode(chip_sum(to_z * 2 + 1 - x))
        x_copy(dz).start()
    for dz in ZORDER:
        to_z = lax.rem(z + dz, 4)
        total = chip_sum(to_z * 2 + x)
        x_copy(dz).wait_recv()
        total = total + decode(x_in[dz])
        if dz:
            z_out[dz] = encode(total)
            z_copy(dz).start()
        else:
            out_ref[...] = total
    for dz in (1, 3, 2):
        z_copy(dz).wait_recv()
        out_ref[...] += decode(z_in[dz])

    for d in ORDER:
        to = lax.rem(me + d, n)
        key_copy(to).wait_send()
        tile_copy(to).wait_send()
    for j in range(4):
        forward(j).wait_send()
    for k in range(4):
        core_copy(0, k).wait_send()
    for dz in range(4):
        x_copy(dz).wait_send()
        if dz:
            z_copy(dz).wait_send()


def fused(amplitudes, integrals, tile_block, tile_index):
    rows = amplitudes.shape[0]
    dma = pltpu.SemaphoreType.DMA
    bf16, f32, i32, i16 = jnp.bfloat16, jnp.float32, jnp.int32, jnp.int16
    return pl.pallas_call(
        kernel,
        out_shape=jax.ShapeDtypeStruct((16, 1024), f32),
        in_specs=[
            pl.BlockSpec(memory_space=pl.ANY),
            pl.BlockSpec(memory_space=pl.ANY),
            pl.BlockSpec(memory_space=pl.ANY),
            pl.BlockSpec(memory_space=pl.ANY),
        ],
        out_specs=pl.BlockSpec(memory_space=pltpu.VMEM),
        scratch_shapes=[
            pltpu.SMEM((rows,), i32),
            pltpu.SMEM((rows,), i32),
            pltpu.VMEM((rows * 16, 128), bf16),
            pltpu.VMEM((768, 1024), bf16),
            pltpu.VMEM((16, 32, 128), bf16),
            pltpu.VMEM((16, 32, 128), bf16),
            pltpu.VMEM((16, 32, 128), bf16),
            pltpu.VMEM((16, 1, 128), i32),
            pltpu.VMEM((16, 1, 128), i32),
            pltpu.VMEM((768, 512), bf16),
            pltpu.VMEM((128, 768), bf16),
            pltpu.VMEM((2, 4, 8, 16, 256), f32),
            pltpu.VMEM((4, 8, 16, 256), f32),
            pltpu.VMEM((4, 16, 1152), i16),
            pltpu.VMEM((4, 16, 1152), i16),
            pltpu.VMEM((4, 16, 1152), i16),
            pltpu.VMEM((4, 16, 1152), i16),
            dma(()), dma(()), dma(()), dma(()),
            dma((16,)), dma((16,)), dma((16,)), dma((16,)), dma((4,)), dma((4,)),
            dma((4,)), dma((4,)), dma((4,)), dma((4,)), dma((4,)), dma((4,)),
        ],
        compiler_params=pltpu.CompilerParams(
            collective_id=0, has_side_effects=True, vmem_limit_bytes=60 * 1024 * 1024
        ),
        name="ladder",
    )(tile_block, tile_index, amplitudes.reshape(rows * 16, 128), integrals)


def solution(mesh):
    count = (mesh.shape["grp"], mesh.shape["own"])

    def run(amplitudes, integrals, tile_block, tile_index):
        sizes = amplitudes.shape + integrals.shape
        small = count == (2, 16) and sizes == (192, 32, 128, 12288, 2048)
        return jax.shard_map(
            fused if small else local,
            mesh=mesh,
            in_specs=(P("own", "grp", None), P("own", "grp"), P("own"), P("own")),
            out_specs=P("own", "grp"),
            check_vma=False,
        )(amplitudes, integrals, tile_block, tile_index)

    return run
```

```python
import functools

import jax
import jax.numpy as jnp
from jax import lax
from jax.experimental import pallas as pl
from jax.experimental.pallas import tpu as pltpu
from jax.sharding import PartitionSpec as P

NB = 8
CAP = 2
MESH = pl.DeviceIdType.MESH
ORDER = (8, 7, 9, 6, 10, 5, 11, 4, 12, 3, 13, 2, 14, 1, 15)


def local(amplitudes, integrals, tile_block, tile_index):
    own_count = lax.axis_size("own")
    tile_width = amplitudes.shape[2]
    tile_dev = integrals.shape[0] // tile_width
    tile_owner = tile_index // tile_dev
    local_tile = tile_index - tile_owner * tile_dev
    tile_key = tile_block * tile_dev + local_tile
    one_hot = (tile_owner[:, None] == jnp.arange(own_count)[None, :]).astype(jnp.int32)
    slot_rank = jnp.sum((jnp.cumsum(one_hot, axis=0) - one_hot) * one_hot, axis=1)
    key_buffer = jnp.full((own_count, CAP), -1, jnp.int32).at[tile_owner, slot_rank].set(tile_key)
    gathered = lax.all_gather(amplitudes, "grp", axis=1, tiled=True)
    buffer = jnp.zeros((own_count, CAP) + gathered.shape[1:], gathered.dtype)
    received = lax.all_to_all(
        buffer.at[tile_owner, slot_rank].set(gathered),
        "own",
        split_axis=0,
        concat_axis=0,
        tiled=True,
    )
    recv_keys = lax.all_to_all(key_buffer, "own", split_axis=0, concat_axis=0, tiled=True)
    occ_rows = received.shape[2]
    slots = received.reshape(own_count * CAP, occ_rows, tile_width)
    flat_keys = recv_keys.reshape(own_count * CAP)
    recv_block = jnp.where(flat_keys >= 0, flat_keys // tile_dev, -1)
    recv_tile = jnp.where(flat_keys >= 0, flat_keys % tile_dev, 0)
    row_count = NB * occ_rows
    row_index = recv_block[:, None] * occ_rows + jnp.arange(occ_rows)[None, :]
    in_range = (recv_block[:, None] >= 0) & (row_index >= 0) & (row_index < row_count)
    row_index = jnp.where(in_range, row_index, row_count)
    tile_slot = jnp.broadcast_to(recv_tile[:, None], row_index.shape)
    placed = jnp.zeros((row_count, tile_dev, tile_width), slots.dtype)
    placed = placed.at[row_index, tile_slot].set(slots, mode="drop")
    return lax.psum_scatter(
        jnp.dot(
            placed.reshape(row_count, tile_dev * tile_width),
            integrals,
            preferred_element_type=jnp.float32,
        ),
        "own",
        scatter_dimension=0,
        tiled=True,
    )


def encode(v):
    parts = [v[:, k * 128 : (k + 1) * 128] for k in range(8)]
    top = functools.reduce(jnp.maximum, [jnp.abs(p) for p in parts])
    expo = jnp.ceil(jnp.log2(jnp.maximum(top, 1e-30)))
    scale = jnp.exp2(15.0 - expo)
    coded = [jnp.clip(jnp.round(p * scale), -32767.0, 32767.0) for p in parts] + [expo]
    return jnp.concatenate(coded, axis=1).astype(jnp.int32).astype(jnp.int16)


def decode(q):
    wide = q.astype(jnp.int32).astype(jnp.float32)
    scale = jnp.exp2(wide[:, 1024:] - 15.0)
    return jnp.concatenate([wide[:, k * 128 : (k + 1) * 128] * scale for k in range(8)], axis=1)


def kernel(
    block_hbm, index_hbm, amp_hbm, int_hbm, out_ref,
    block_ref, index_ref, amp_ref, ints, sends, recvs, others, key_out, key_in, pick, lhs, prod, sib,
    x_out, x_in, z_out, z_in,
    int_sem, amp_sem, block_sem, index_sem, tile_ss, tile_rs, key_ss, key_rs, fwd_ss, fwd_rs,
    core_ss, core_rs, x_ss, x_rs, z_ss, z_rs,
):
    n = 16
    rows = amp_ref.shape[0] // 16
    tile_dev = 6
    me = lax.axis_index("own")
    g = lax.axis_index("grp")
    core = lax.rem(me, 2)
    x = lax.rem(me // 2, 2)
    z = me // 4
    sibling = me + 1 - 2 * core
    across = me + 2 - 4 * x

    load_index = pltpu.make_async_copy(index_hbm, index_ref, index_sem)
    load_block = pltpu.make_async_copy(block_hbm, block_ref, block_sem)
    load_amp = pltpu.make_async_copy(amp_hbm, amp_ref, amp_sem)
    load = pltpu.make_async_copy(int_hbm, ints, int_sem)
    load_index.start()
    load_block.start()
    load_amp.start()
    barrier = pltpu.get_barrier_semaphore()
    for d in range(1, n):
        pl.semaphore_signal(barrier, inc=1, device_id={"own": lax.rem(me + d, n)}, device_id_type=MESH)
    pl.semaphore_signal(barrier, inc=1, device_id={"grp": 1 - g}, device_id_type=MESH)

    load.start()
    load_index.wait()
    load_block.wait()

    owner, rank, key = [], [], []
    for r in range(rows):
        t = index_ref[r]
        o = t // tile_dev
        owner.append(o)
        key.append((t - o * tile_dev) * NB + block_ref[r])
        earlier = jnp.int32(0)
        for q in range(r):
            earlier = earlier + jnp.where(owner[q] == o, 1, 0)
        rank.append(earlier)

    dest = lax.broadcasted_iota(jnp.int32, (n, 128), 0)
    lane = lax.broadcasted_iota(jnp.int32, (n, 128), 1)
    sub = lane - lax.rem(me, 4) * 32
    slot = jnp.where((sub >= 0) & (sub < 32), dest * 2 + sub // 16, -1)
    inner = lax.rem(lane, 16)
    keys = jnp.zeros((n, 128), jnp.int32)
    for r in range(rows):
        keys = keys + jnp.where(slot == owner[r] * 2 + rank[r], key[r] * 16 + inner + 1, 0)
    for o in range(n):
        key_out[o] = keys[o : o + 1, :]

    col = lax.broadcasted_iota(jnp.int32, (1, rows * 16), 1)
    place = jnp.zeros((1, rows * 16), jnp.int32)
    for r in range(rows):
        place = jnp.where(col // 16 == r, (owner[r] * 2 + rank[r]) * 16 + lax.rem(col, 16), place)
    load_amp.wait()
    amp = amp_ref[...]
    for part in range(4):
        row = lax.broadcasted_iota(jnp.int32, (128, rows * 16), 0) + part * 128
        hot = jnp.where(row == place, 1.0, 0.0).astype(jnp.bfloat16)
        got = jnp.dot(hot, amp, preferred_element_type=jnp.float32).astype(jnp.bfloat16)
        sends[pl.ds(part * 4, 4)] = got.reshape(4, 32, 128)
    recvs[me] = sends[me]
    key_in[me] = key_out[me]

    pl.semaphore_wait(barrier, n)

    def key_copy(to):
        return pltpu.make_async_remote_copy(
            key_out.at[to], key_in.at[me], key_ss.at[to], key_rs.at[me],
            device_id={"own": to}, device_id_type=MESH,
        )

    def tile_copy(to):
        return pltpu.make_async_remote_copy(
            sends.at[to], recvs.at[me], tile_ss.at[to], tile_rs.at[me],
            device_id={"own": to}, device_id_type=MESH,
        )

    def forward(j):
        return pltpu.make_async_remote_copy(
            recvs.at[pl.ds(j * 4, 4)], others.at[pl.ds(j * 4, 4)], fwd_ss.at[j], fwd_rs.at[j],
            device_id={"grp": 1 - g}, device_id_type=MESH,
        )

    for d in ORDER:
        key_copy(lax.rem(me + d, n)).start()
    for d in ORDER:
        tile_copy(lax.rem(me + d, n)).start()

    def arrived(s, buffer, sem):
        return pltpu.make_async_remote_copy(
            buffer.at[s], buffer.at[s], sem.at[s], sem.at[s],
            device_id={"own": sibling}, device_id_type=MESH,
        )

    for d in ORDER:
        arrived(lax.rem(me + n - d, n), key_in, key_rs).wait_recv()
    targets = [
        key_in[4 * j] + key_in[4 * j + 1] + key_in[4 * j + 2] + key_in[4 * j + 3] for j in range(4)
    ]
    target = jnp.concatenate(targets, axis=1)
    for t in range(tile_dev):
        row = lax.broadcasted_iota(jnp.int32, (128, 512), 0) + (t * 128 + 1)
        pick[t * 128 : (t + 1) * 128, :] = jnp.where(row == target, 1.0, 0.0).astype(jnp.bfloat16)

    for dz in (0, 1, 3, 2):
        j = lax.rem(z + dz, 4)
        for w in range(4):
            if dz or w:
                arrived(j * 4 + lax.rem(me + w, 4), recvs, tile_rs).wait_recv()
        forward(j).start()

    def place(source):
        tiles = source[...].reshape(512, 128)
        got = jnp.dot(pick[...], tiles, preferred_element_type=jnp.float32).astype(jnp.bfloat16)
        for t in range(tile_dev):
            lhs[:, t * 128 : (t + 1) * 128] = got[t * 128 : (t + 1) * 128]

    def core_copy(h, k):
        return pltpu.make_async_remote_copy(
            prod.at[h, k, pl.ds(4 * (1 - core), 4)], sib.at[h, k], core_ss.at[h, k], core_rs.at[h, k],
            device_id={"own": sibling}, device_id_type=MESH,
        )

    def multiply(h):
        for k in range(4):
            prod[h, k] = jnp.dot(
                lhs[...], ints[:, k * 256 : (k + 1) * 256], preferred_element_type=jnp.float32
            ).reshape(8, 16, 256)
            core_copy(h, k).start()

    def chip_sum(h, b):
        return jnp.concatenate(
            [prod[h, k, 4 * core + b] + sib[h, k, b] for k in range(4)], axis=1
        )

    def x_copy(h, j):
        return pltpu.make_async_remote_copy(
            x_out.at[h, j], x_in.at[h, j], x_ss.at[h, j], x_rs.at[h, j],
            device_id={"own": across}, device_id_type=MESH,
        )

    def z_copy(h, j):
        target = 4 * (2 * core + j) + 2 * x + (g if h == 0 else 1 - g)
        return pltpu.make_async_remote_copy(
            z_out.at[h, j], z_in.at[z], z_ss.at[h, j], z_rs.at[z],
            device_id={"own": target}, device_id_type=MESH,
        )

    def stays(h, j):
        return jnp.logical_and(z == 2 * core + j, core == (g if h == 0 else 1 - g))

    def x_phase(h):
        for k in range(4):
            core_copy(h, k).wait_recv()
        for j in range(2):
            x_out[h, j] = encode(chip_sum(h, 2 * j + 1 - x))
            x_copy(h, j).start()

    def z_phase(h):
        for j in range(2):
            x_copy(h, j).wait_recv()
            total = chip_sum(h, 2 * j + x) + decode(x_in[h, j])

            @pl.when(stays(h, j))
            def _():
                out_ref[...] = total

            @pl.when(jnp.logical_not(stays(h, j)))
            def _():
                z_out[h, j] = encode(total)
                z_copy(h, j).start()

    place(recvs)
    load.wait()
    multiply(0)
    for j in range(4):
        forward(j).wait_recv()
    place(others)
    x_phase(0)
    multiply(1)
    z_phase(0)
    x_phase(1)
    z_phase(1)

    @pl.when(z // 2 != core)
    def _():
        arrived(z, z_in, z_rs).wait_recv()
        out_ref[...] = decode(z_in[z])

    for dz in (1, 3, 2):
        source = lax.rem(z + dz, 4)
        arrived(source, z_in, z_rs).wait_recv()
        out_ref[...] += decode(z_in[source])

    for d in ORDER:
        to = lax.rem(me + d, n)
        key_copy(to).wait_send()
        tile_copy(to).wait_send()
    for j in range(4):
        forward(j).wait_send()
    for h in range(2):
        for k in range(4):
            core_copy(h, k).wait_send()
        for j in range(2):
            x_copy(h, j).wait_send()

            @pl.when(jnp.logical_not(stays(h, j)))
            def _():
                z_copy(h, j).wait_send()


def fused(amplitudes, integrals, tile_block, tile_index):
    rows = amplitudes.shape[0]
    dma = pltpu.SemaphoreType.DMA
    bf16, f32, i32, i16 = jnp.bfloat16, jnp.float32, jnp.int32, jnp.int16
    return pl.pallas_call(
        kernel,
        out_shape=jax.ShapeDtypeStruct((16, 1024), f32),
        in_specs=[
            pl.BlockSpec(memory_space=pl.ANY),
            pl.BlockSpec(memory_space=pl.ANY),
            pl.BlockSpec(memory_space=pl.ANY),
            pl.BlockSpec(memory_space=pl.ANY),
        ],
        out_specs=pl.BlockSpec(memory_space=pltpu.VMEM),
        scratch_shapes=[
            pltpu.SMEM((rows,), i32),
            pltpu.SMEM((rows,), i32),
            pltpu.VMEM((rows * 16, 128), bf16),
            pltpu.VMEM((768, 1024), bf16),
            pltpu.VMEM((16, 32, 128), bf16),
            pltpu.VMEM((16, 32, 128), bf16),
            pltpu.VMEM((16, 32, 128), bf16),
            pltpu.VMEM((16, 1, 128), i32),
            pltpu.VMEM((16, 1, 128), i32),
            pltpu.VMEM((768, 512), bf16),
            pltpu.VMEM((128, 768), bf16),
            pltpu.VMEM((2, 4, 8, 16, 256), f32),
            pltpu.VMEM((2, 4, 4, 16, 256), f32),
            pltpu.VMEM((2, 2, 16, 1152), i16),
            pltpu.VMEM((2, 2, 16, 1152), i16),
            pltpu.VMEM((2, 2, 16, 1152), i16),
            pltpu.VMEM((4, 16, 1152), i16),
            dma(()), dma(()), dma(()), dma(()),
            dma((16,)), dma((16,)), dma((16,)), dma((16,)), dma((4,)), dma((4,)),
            dma((2, 4)), dma((2, 4)), dma((2, 2)), dma((2, 2)), dma((2, 2)), dma((4,)),
        ],
        compiler_params=pltpu.CompilerParams(
            collective_id=0, has_side_effects=True, vmem_limit_bytes=60 * 1024 * 1024
        ),
        name="ladder",
    )(tile_block, tile_index, amplitudes.reshape(rows * 16, 128), integrals)


def solution(mesh):
    count = (mesh.shape["grp"], mesh.shape["own"])

    def run(amplitudes, integrals, tile_block, tile_index):
        sizes = amplitudes.shape + integrals.shape
        small = count == (2, 16) and sizes == (192, 32, 128, 12288, 2048)
        return jax.shard_map(
            fused if small else local,
            mesh=mesh,
            in_specs=(P("own", "grp", None), P("own", "grp"), P("own"), P("own")),
            out_specs=P("own", "grp"),
            check_vma=False,
        )(amplitudes, integrals, tile_block, tile_index)

    return run
```

```python
import functools

import jax
import jax.numpy as jnp
from jax import lax
from jax.experimental import pallas as pl
from jax.experimental.pallas import tpu as pltpu
from jax.sharding import PartitionSpec as P

NB = 8
CAP = 2
MESH = pl.DeviceIdType.MESH


def loop(count):
    def run(body):
        lax.fori_loop(0, count, lambda i, carry: (body(i), carry)[1], 0)

    return run


def local(amplitudes, integrals, tile_block, tile_index):
    own_count = lax.axis_size("own")
    tile_width = amplitudes.shape[2]
    tile_dev = integrals.shape[0] // tile_width
    tile_owner = tile_index // tile_dev
    local_tile = tile_index - tile_owner * tile_dev
    tile_key = tile_block * tile_dev + local_tile
    one_hot = (tile_owner[:, None] == jnp.arange(own_count)[None, :]).astype(jnp.int32)
    slot_rank = jnp.sum((jnp.cumsum(one_hot, axis=0) - one_hot) * one_hot, axis=1)
    key_buffer = jnp.full((own_count, CAP), -1, jnp.int32).at[tile_owner, slot_rank].set(tile_key)
    gathered = lax.all_gather(amplitudes, "grp", axis=1, tiled=True)
    buffer = jnp.zeros((own_count, CAP) + gathered.shape[1:], gathered.dtype)
    received = lax.all_to_all(
        buffer.at[tile_owner, slot_rank].set(gathered),
        "own",
        split_axis=0,
        concat_axis=0,
        tiled=True,
    )
    recv_keys = lax.all_to_all(key_buffer, "own", split_axis=0, concat_axis=0, tiled=True)
    occ_rows = received.shape[2]
    slots = received.reshape(own_count * CAP, occ_rows, tile_width)
    flat_keys = recv_keys.reshape(own_count * CAP)
    recv_block = jnp.where(flat_keys >= 0, flat_keys // tile_dev, -1)
    recv_tile = jnp.where(flat_keys >= 0, flat_keys % tile_dev, 0)
    row_count = NB * occ_rows
    row_index = recv_block[:, None] * occ_rows + jnp.arange(occ_rows)[None, :]
    in_range = (recv_block[:, None] >= 0) & (row_index >= 0) & (row_index < row_count)
    row_index = jnp.where(in_range, row_index, row_count)
    tile_slot = jnp.broadcast_to(recv_tile[:, None], row_index.shape)
    placed = jnp.zeros((row_count, tile_dev, tile_width), slots.dtype)
    placed = placed.at[row_index, tile_slot].set(slots, mode="drop")
    return lax.psum_scatter(
        jnp.dot(
            placed.reshape(row_count, tile_dev * tile_width),
            integrals,
            preferred_element_type=jnp.float32,
        ),
        "own",
        scatter_dimension=0,
        tiled=True,
    )


def encode(v):
    parts = [v[:, k * 128 : (k + 1) * 128] for k in range(8)]
    top = functools.reduce(jnp.maximum, [jnp.abs(p) for p in parts])
    expo = jnp.ceil(jnp.log2(jnp.maximum(top, 1e-30)))
    scale = jnp.exp2(15.0 - expo)
    coded = [jnp.clip(jnp.round(p * scale), -32767.0, 32767.0) for p in parts] + [expo]
    return jnp.concatenate(coded, axis=1).astype(jnp.int32).astype(jnp.int16)


def decode(q):
    wide = q.astype(jnp.int32).astype(jnp.float32)
    scale = jnp.exp2(wide[:, 1024:] - 15.0)
    return jnp.concatenate([wide[:, k * 128 : (k + 1) * 128] * scale for k in range(8)], axis=1)


def kernel(
    block_hbm, index_hbm, amp_hbm, int_hbm, out_ref,
    block_ref, index_ref, amp_ref, ints, sends, tiles, key_out, key_in, pick, lhs, prod, sib,
    x_out, x_in, z_out, z_in,
    int_sem, amp_sem, block_sem, index_sem, tile_ss, tile_rs, key_ss, key_rs, fwd_ss, fwd_rs,
    core_ss, core_rs, x_ss, x_rs, z_ss, z_rs,
):
    n = 16
    rows = amp_ref.shape[0] // 16
    tile_dev = 6
    me = lax.axis_index("own")
    g = lax.axis_index("grp")
    core = lax.rem(me, 2)
    x = lax.rem(me // 2, 2)
    z = me // 4
    sibling = me + 1 - 2 * core
    across = me + 2 - 4 * x

    load_index = pltpu.make_async_copy(index_hbm, index_ref, index_sem)
    load_block = pltpu.make_async_copy(block_hbm, block_ref, block_sem)
    load_amp = pltpu.make_async_copy(amp_hbm, amp_ref, amp_sem)
    load = pltpu.make_async_copy(int_hbm, ints, int_sem)
    load_index.start()
    load_block.start()
    load_amp.start()
    barrier = pltpu.get_barrier_semaphore()

    @loop(n - 1)
    def _(i):
        pl.semaphore_signal(barrier, inc=1, device_id={"own": lax.rem(me + i + 1, n)}, device_id_type=MESH)

    pl.semaphore_signal(barrier, inc=1, device_id={"grp": 1 - g}, device_id_type=MESH)

    load.start()
    load_index.wait()
    load_block.wait()

    owner, rank, key = [], [], []
    for r in range(rows):
        t = index_ref[r]
        o = t // tile_dev
        owner.append(o)
        key.append((t - o * tile_dev) * NB + block_ref[r])
        earlier = jnp.int32(0)
        for q in range(r):
            earlier = earlier + jnp.where(owner[q] == o, 1, 0)
        rank.append(earlier)

    dest = lax.broadcasted_iota(jnp.int32, (n, 128), 0)
    lane = lax.broadcasted_iota(jnp.int32, (n, 128), 1)
    sub = lane - lax.rem(me, 4) * 32
    slot = jnp.where((sub >= 0) & (sub < 32), dest * 2 + sub // 16, -1)
    inner = lax.rem(lane, 16)
    keys = jnp.zeros((n, 128), jnp.int32)
    for r in range(rows):
        keys = keys + jnp.where(slot == owner[r] * 2 + rank[r], key[r] * 16 + inner + 1, 0)
    for o in range(n):
        key_out[o] = keys[o : o + 1, :]

    col = lax.broadcasted_iota(jnp.int32, (1, rows * 16), 1)
    place = jnp.zeros((1, rows * 16), jnp.int32)
    for r in range(rows):
        place = jnp.where(col // 16 == r, (owner[r] * 2 + rank[r]) * 16 + lax.rem(col, 16), place)
    load_amp.wait()
    amp = amp_ref[...]

    @loop(4)
    def _(part):
        row = lax.broadcasted_iota(jnp.int32, (128, rows * 16), 0)
        hot = jnp.where(row == place - part * 128, 1.0, 0.0).astype(jnp.bfloat16)
        got = jnp.dot(hot, amp, preferred_element_type=jnp.float32).astype(jnp.bfloat16)
        sends[pl.ds(part * 4, 4)] = got.reshape(4, 32, 128)

    tiles[0, me] = sends[me]
    key_in[me] = key_out[me]

    pl.semaphore_wait(barrier, n)

    def key_copy(to):
        return pltpu.make_async_remote_copy(
            key_out.at[to], key_in.at[me], key_ss.at[to], key_rs.at[me],
            device_id={"own": to}, device_id_type=MESH,
        )

    def tile_copy(to):
        return pltpu.make_async_remote_copy(
            sends.at[to], tiles.at[0, me], tile_ss.at[to], tile_rs.at[me],
            device_id={"own": to}, device_id_type=MESH,
        )

    def forward(j):
        return pltpu.make_async_remote_copy(
            tiles.at[0, pl.ds(j * 4, 4)], tiles.at[1, pl.ds(j * 4, 4)], fwd_ss.at[j], fwd_rs.at[j],
            device_id={"grp": 1 - g}, device_id_type=MESH,
        )

    def others(body):
        @loop(n)
        def _(i):
            to = lax.rem(z + 2 + i // 4, 4) * 4 + lax.rem(me + i, 4)

            @pl.when(to != me)
            def _():
                body(to)

    others(lambda to: key_copy(to).start())
    others(lambda to: tile_copy(to).start())

    def arrived(s, buffer, sem):
        return pltpu.make_async_remote_copy(
            buffer.at[s], buffer.at[s], sem.at[s], sem.at[s],
            device_id={"own": sibling}, device_id_type=MESH,
        )

    others(lambda s: arrived(s, key_in, key_rs).wait_recv())
    targets = [
        key_in[4 * j] + key_in[4 * j + 1] + key_in[4 * j + 2] + key_in[4 * j + 3] for j in range(4)
    ]
    target = jnp.concatenate(targets, axis=1)

    @loop(tile_dev)
    def _(t):
        row = lax.broadcasted_iota(jnp.int32, (128, 512), 0)
        pick[pl.ds(pl.multiple_of(t * 128, 128), 128), :] = jnp.where(
            row == target - (t * 128 + 1), 1.0, 0.0
        ).astype(jnp.bfloat16)

    @loop(4)
    def _(i):
        j = lax.rem(z + i, 4)

        @loop(4)
        def _(w):
            s = j * 4 + w

            @pl.when(s != me)
            def _():
                arrived(s, tiles.at[0], tile_rs).wait_recv()

        forward(j).start()

    def place(h):
        slots = tiles[h].reshape(512, 128)
        for t in range(tile_dev):
            lhs[:, t * 128 : (t + 1) * 128] = jnp.dot(
                pick[t * 128 : (t + 1) * 128, :], slots, preferred_element_type=jnp.float32
            ).astype(jnp.bfloat16)

    def core_copy(h, k):
        return pltpu.make_async_remote_copy(
            prod.at[h, k, pl.ds(4 * (1 - core), 4)], sib.at[h, k], core_ss.at[h, k], core_rs.at[h, k],
            device_id={"own": sibling}, device_id_type=MESH,
        )

    def multiply(h):
        @loop(4)
        def _(k):
            cols = pl.ds(pl.multiple_of(k * 256, 256), 256)
            prod[h, k] = jnp.dot(
                lhs[...], ints[:, cols], preferred_element_type=jnp.float32
            ).reshape(8, 16, 256)
            core_copy(h, k).start()

    def chip_sum(h, b):
        return jnp.concatenate(
            [prod[h, k, 4 * core + b] + sib[h, k, b] for k in range(4)], axis=1
        )

    def x_copy(h, j):
        return pltpu.make_async_remote_copy(
            x_out.at[h, j], x_in.at[h, j], x_ss.at[h, j], x_rs.at[h, j],
            device_id={"own": across}, device_id_type=MESH,
        )

    def z_copy(h, j):
        target = 4 * (2 * core + j) + 2 * x + lax.rem(g + h, 2)
        return pltpu.make_async_remote_copy(
            z_out.at[h, j], z_in.at[z], z_ss.at[h, j], z_rs.at[z],
            device_id={"own": target}, device_id_type=MESH,
        )

    def stays(h, j):
        return jnp.logical_and(z == 2 * core + j, core == lax.rem(g + h, 2))

    def x_phase(h):
        for k in range(4):
            core_copy(h, k).wait_recv()

        @loop(2)
        def _(j):
            x_out[h, j] = encode(chip_sum(h, 2 * j + 1 - x))
            x_copy(h, j).start()

    def z_phase(h, j):
        x_copy(h, j).wait_recv()
        total = chip_sum(h, 2 * j + x) + decode(x_in[h, j])

        @pl.when(stays(h, j))
        def _():
            out_ref[...] = total

        @pl.when(jnp.logical_not(stays(h, j)))
        def _():
            z_out[h, j] = encode(total)
            z_copy(h, j).start()

    load.wait()

    @loop(3)
    def _(i):
        @pl.when(i < 2)
        def _():
            @pl.when(i == 1)
            def _():
                for j in range(4):
                    forward(j).wait_recv()

            place(i)
            multiply(i)

        @pl.when(i > 0)
        def _():
            x_phase(i - 1)

    @loop(4)
    def _(i):
        z_phase(i // 2, lax.rem(i, 2))

    @pl.when(z // 2 != core)
    def _():
        arrived(z, z_in, z_rs).wait_recv()
        out_ref[...] = decode(z_in[z])

    @loop(3)
    def _(i):
        source = lax.rem(z + i + 1, 4)
        arrived(source, z_in, z_rs).wait_recv()
        out_ref[...] += decode(z_in[source])

    @others
    def _(to):
        key_copy(to).wait_send()
        tile_copy(to).wait_send()

    for j in range(4):
        forward(j).wait_send()

    @loop(2)
    def _(h):
        for k in range(4):
            core_copy(h, k).wait_send()

        @loop(2)
        def _(j):
            x_copy(h, j).wait_send()

            @pl.when(jnp.logical_not(stays(h, j)))
            def _():
                z_copy(h, j).wait_send()


def fused(amplitudes, integrals, tile_block, tile_index):
    rows = amplitudes.shape[0]
    dma = pltpu.SemaphoreType.DMA
    bf16, f32, i32, i16 = jnp.bfloat16, jnp.float32, jnp.int32, jnp.int16
    return pl.pallas_call(
        kernel,
        out_shape=jax.ShapeDtypeStruct((16, 1024), f32),
        in_specs=[
            pl.BlockSpec(memory_space=pl.ANY),
            pl.BlockSpec(memory_space=pl.ANY),
            pl.BlockSpec(memory_space=pl.ANY),
            pl.BlockSpec(memory_space=pl.ANY),
        ],
        out_specs=pl.BlockSpec(memory_space=pltpu.VMEM),
        scratch_shapes=[
            pltpu.SMEM((rows,), i32),
            pltpu.SMEM((rows,), i32),
            pltpu.VMEM((rows * 16, 128), bf16),
            pltpu.VMEM((768, 1024), bf16),
            pltpu.VMEM((16, 32, 128), bf16),
            pltpu.VMEM((2, 16, 32, 128), bf16),
            pltpu.VMEM((16, 1, 128), i32),
            pltpu.VMEM((16, 1, 128), i32),
            pltpu.VMEM((768, 512), bf16),
            pltpu.VMEM((128, 768), bf16),
            pltpu.VMEM((2, 4, 8, 16, 256), f32),
            pltpu.VMEM((2, 4, 4, 16, 256), f32),
            pltpu.VMEM((2, 2, 16, 1152), i16),
            pltpu.VMEM((2, 2, 16, 1152), i16),
            pltpu.VMEM((2, 2, 16, 1152), i16),
            pltpu.VMEM((4, 16, 1152), i16),
            dma(()), dma(()), dma(()), dma(()),
            dma((16,)), dma((16,)), dma((16,)), dma((16,)), dma((4,)), dma((4,)),
            dma((2, 4)), dma((2, 4)), dma((2, 2)), dma((2, 2)), dma((2, 2)), dma((4,)),
        ],
        compiler_params=pltpu.CompilerParams(
            collective_id=0, has_side_effects=True, vmem_limit_bytes=60 * 1024 * 1024
        ),
        name="ladder",
    )(tile_block, tile_index, amplitudes.reshape(rows * 16, 128), integrals)


def solution(mesh):
    count = (mesh.shape["grp"], mesh.shape["own"])

    def run(amplitudes, integrals, tile_block, tile_index):
        sizes = amplitudes.shape + integrals.shape
        small = count == (2, 16) and sizes == (192, 32, 128, 12288, 2048)
        return jax.shard_map(
            fused if small else local,
            mesh=mesh,
            in_specs=(P("own", "grp", None), P("own", "grp"), P("own"), P("own")),
            out_specs=P("own", "grp"),
            check_vma=False,
        )(amplitudes, integrals, tile_block, tile_index)

    return run
```

```python
import functools

import jax
import jax.numpy as jnp
from jax import lax
from jax.experimental import pallas as pl
from jax.experimental.pallas import tpu as pltpu
from jax.sharding import PartitionSpec as P

NB = 8
CAP = 2
MESH = pl.DeviceIdType.MESH


def loop(count):
    def run(body):
        lax.fori_loop(0, count, lambda i, carry: (body(i), carry)[1], 0)

    return run


def local(amplitudes, integrals, tile_block, tile_index):
    own_count = lax.axis_size("own")
    tile_width = amplitudes.shape[2]
    tile_dev = integrals.shape[0] // tile_width
    tile_owner = tile_index // tile_dev
    local_tile = tile_index - tile_owner * tile_dev
    tile_key = tile_block * tile_dev + local_tile
    one_hot = (tile_owner[:, None] == jnp.arange(own_count)[None, :]).astype(jnp.int32)
    slot_rank = jnp.sum((jnp.cumsum(one_hot, axis=0) - one_hot) * one_hot, axis=1)
    key_buffer = jnp.full((own_count, CAP), -1, jnp.int32).at[tile_owner, slot_rank].set(tile_key)
    gathered = lax.all_gather(amplitudes, "grp", axis=1, tiled=True)
    buffer = jnp.zeros((own_count, CAP) + gathered.shape[1:], gathered.dtype)
    received = lax.all_to_all(
        buffer.at[tile_owner, slot_rank].set(gathered),
        "own",
        split_axis=0,
        concat_axis=0,
        tiled=True,
    )
    recv_keys = lax.all_to_all(key_buffer, "own", split_axis=0, concat_axis=0, tiled=True)
    occ_rows = received.shape[2]
    slots = received.reshape(own_count * CAP, occ_rows, tile_width)
    flat_keys = recv_keys.reshape(own_count * CAP)
    recv_block = jnp.where(flat_keys >= 0, flat_keys // tile_dev, -1)
    recv_tile = jnp.where(flat_keys >= 0, flat_keys % tile_dev, 0)
    row_count = NB * occ_rows
    row_index = recv_block[:, None] * occ_rows + jnp.arange(occ_rows)[None, :]
    in_range = (recv_block[:, None] >= 0) & (row_index >= 0) & (row_index < row_count)
    row_index = jnp.where(in_range, row_index, row_count)
    tile_slot = jnp.broadcast_to(recv_tile[:, None], row_index.shape)
    placed = jnp.zeros((row_count, tile_dev, tile_width), slots.dtype)
    placed = placed.at[row_index, tile_slot].set(slots, mode="drop")
    return lax.psum_scatter(
        jnp.dot(
            placed.reshape(row_count, tile_dev * tile_width),
            integrals,
            preferred_element_type=jnp.float32,
        ),
        "own",
        scatter_dimension=0,
        tiled=True,
    )


def encode(v):
    parts = [v[:, k * 128 : (k + 1) * 128] for k in range(8)]
    top = functools.reduce(jnp.maximum, [jnp.abs(p) for p in parts])
    expo = jnp.ceil(jnp.log2(jnp.maximum(top, 1e-30)))
    scale = jnp.exp2(15.0 - expo)
    coded = [jnp.clip(jnp.round(p * scale), -32767.0, 32767.0) for p in parts] + [expo]
    return jnp.concatenate(coded, axis=1).astype(jnp.int32).astype(jnp.int16)


def decode(q):
    wide = q.astype(jnp.int32).astype(jnp.float32)
    scale = jnp.exp2(wide[:, 1024:] - 15.0)
    return jnp.concatenate([wide[:, k * 128 : (k + 1) * 128] * scale for k in range(8)], axis=1)


def kernel(
    block_hbm, index_hbm, amp_hbm, int_hbm, out_ref,
    block_ref, index_ref, amp_ref, ints, sends, tiles, key_out, key_in, pick, lhs, prod, sib,
    coded, landed,
    int_sem, amp_sem, block_sem, index_sem, tile_ss, tile_rs, key_ss, key_rs, fwd_ss, fwd_rs,
    core_ss, core_rs, sum_ss, sum_rs,
):
    n = 16
    rows = amp_ref.shape[0] // 16
    tile_dev = 6
    me = lax.axis_index("own")
    g = lax.axis_index("grp")
    core = lax.rem(me, 2)
    z = me // 4
    sibling = me + 1 - 2 * core

    load_index = pltpu.make_async_copy(index_hbm, index_ref, index_sem)
    load_block = pltpu.make_async_copy(block_hbm, block_ref, block_sem)
    load_amp = pltpu.make_async_copy(amp_hbm, amp_ref, amp_sem)
    load = pltpu.make_async_copy(int_hbm, ints, int_sem)
    load_index.start()
    load_block.start()
    load_amp.start()
    barrier = pltpu.get_barrier_semaphore()

    @loop(n - 1)
    def _(i):
        pl.semaphore_signal(barrier, inc=1, device_id={"own": lax.rem(me + i + 1, n)}, device_id_type=MESH)

    pl.semaphore_signal(barrier, inc=1, device_id={"grp": 1 - g}, device_id_type=MESH)

    load.start()
    load_index.wait()
    load_block.wait()

    owner, rank, key = [], [], []
    for r in range(rows):
        t = index_ref[r]
        o = t // tile_dev
        owner.append(o)
        key.append((t - o * tile_dev) * NB + block_ref[r])
        earlier = jnp.int32(0)
        for q in range(r):
            earlier = earlier + jnp.where(owner[q] == o, 1, 0)
        rank.append(earlier)

    dest = lax.broadcasted_iota(jnp.int32, (n, 128), 0)
    lane = lax.broadcasted_iota(jnp.int32, (n, 128), 1)
    sub = lane - lax.rem(me, 4) * 32
    slot = jnp.where((sub >= 0) & (sub < 32), dest * 2 + sub // 16, -1)
    inner = lax.rem(lane, 16)
    keys = jnp.zeros((n, 128), jnp.int32)
    for r in range(rows):
        keys = keys + jnp.where(slot == owner[r] * 2 + rank[r], key[r] * 16 + inner + 1, 0)
    for o in range(n):
        key_out[o] = keys[o : o + 1, :]

    col = lax.broadcasted_iota(jnp.int32, (1, rows * 16), 1)
    place_row = jnp.zeros((1, rows * 16), jnp.int32)
    for r in range(rows):
        place_row = jnp.where(col // 16 == r, (owner[r] * 2 + rank[r]) * 16 + lax.rem(col, 16), place_row)
    load_amp.wait()
    amp = amp_ref[...]

    row = lax.broadcasted_iota(jnp.int32, (512, rows * 16), 0)
    hot = jnp.where(row == place_row, 1.0, 0.0).astype(jnp.bfloat16)
    sends[...] = jnp.dot(hot, amp, preferred_element_type=jnp.float32).astype(jnp.bfloat16).reshape(16, 32, 128)
    tiles[0, me] = sends[me]
    key_in[me] = key_out[me]

    pl.semaphore_wait(barrier, n)

    def key_copy(to):
        return pltpu.make_async_remote_copy(
            key_out.at[to], key_in.at[me], key_ss.at[to], key_rs.at[me],
            device_id={"own": to}, device_id_type=MESH,
        )

    def tile_copy(to):
        return pltpu.make_async_remote_copy(
            sends.at[to], tiles.at[0, me], tile_ss.at[to], tile_rs.at[me],
            device_id={"own": to}, device_id_type=MESH,
        )

    def forward(j):
        return pltpu.make_async_remote_copy(
            tiles.at[0, pl.ds(j * 4, 4)], tiles.at[1, pl.ds(j * 4, 4)], fwd_ss.at[j], fwd_rs.at[j],
            device_id={"grp": 1 - g}, device_id_type=MESH,
        )

    def others(body):
        @loop(n)
        def _(i):
            to = lax.rem(z + 2 + i // 4, 4) * 4 + lax.rem(me + i, 4)

            @pl.when(to != me)
            def _():
                body(to)

    others(lambda to: key_copy(to).start())
    others(lambda to: tile_copy(to).start())

    def arrived(s, buffer, sem):
        return pltpu.make_async_remote_copy(
            buffer.at[s], buffer.at[s], sem.at[s], sem.at[s],
            device_id={"own": sibling}, device_id_type=MESH,
        )

    others(lambda s: arrived(s, key_in, key_rs).wait_recv())
    targets = [
        key_in[4 * j] + key_in[4 * j + 1] + key_in[4 * j + 2] + key_in[4 * j + 3] for j in range(4)
    ]
    target = jnp.concatenate(targets, axis=1)

    @loop(tile_dev)
    def _(t):
        row = lax.broadcasted_iota(jnp.int32, (128, 512), 0)
        pick[pl.ds(pl.multiple_of(t * 128, 128), 128), :] = jnp.where(
            row == target - (t * 128 + 1), 1.0, 0.0
        ).astype(jnp.bfloat16)

    @loop(4)
    def _(i):
        j = lax.rem(z + i, 4)

        @loop(4)
        def _(w):
            s = j * 4 + w

            @pl.when(s != me)
            def _():
                arrived(s, tiles.at[0], tile_rs).wait_recv()

        forward(j).start()

    def place(h):
        slots = tiles[h].reshape(512, 128)
        got = jnp.dot(pick[...], slots, preferred_element_type=jnp.float32).astype(jnp.bfloat16)
        for t in range(tile_dev):
            lhs[:, t * 128 : (t + 1) * 128] = got[t * 128 : (t + 1) * 128]

    def core_copy(h, k):
        return pltpu.make_async_remote_copy(
            prod.at[h, k, pl.ds(4 * (1 - core), 4)], sib.at[h, k], core_ss.at[h, k], core_rs.at[h, k],
            device_id={"own": sibling}, device_id_type=MESH,
        )

    def multiply(h, k):
        cols = pl.ds(pl.multiple_of(k * 256, 256), 256)
        prod[h, k] = jnp.dot(
            lhs[...], ints[:, cols], preferred_element_type=jnp.float32
        ).reshape(8, 16, 256)

    def chip_sum(h, b):
        return jnp.concatenate(
            [prod[h, k, 4 * core + b] + sib[h, k, b] for k in range(4)], axis=1
        )

    def send_to(h, q):
        return 8 * core + 2 * q + lax.rem(g + h, 2)

    def sum_copy(h, q):
        return pltpu.make_async_remote_copy(
            coded.at[h, q], landed.at[me // 2], sum_ss.at[h, q], sum_rs.at[me // 2],
            device_id={"own": send_to(h, q)}, device_id_type=MESH,
        )

    def prepare(h, q):
        total = chip_sum(h, q)
        coded[h, q] = encode(total)
        out_ref[...] += jnp.where(send_to(h, q) == me, total, 0.0)

    def send(h, q):
        @pl.when(send_to(h, q) != me)
        def _():
            sum_copy(h, q).start()

    out_ref[...] = jnp.zeros_like(out_ref)
    load.wait()
    place(0)

    @loop(4)
    def _(k):
        multiply(0, k)
        core_copy(0, k).start()

    for j in range(4):
        forward(j).wait_recv()
    place(1)
    for k in range(4):
        core_copy(0, k).wait_recv()

    @loop(4)
    def _(k):
        prepare(0, k)
        multiply(1, k)
        core_copy(1, k).start()
        send(0, k)

    for k in range(4):
        core_copy(1, k).wait_recv()

    @loop(4)
    def _(k):
        prepare(1, k)
        send(1, k)

    @loop(8)
    def _(i):
        source = lax.rem(me // 2 + i, 8)

        @pl.when(jnp.logical_or(i > 0, z // 2 != core))
        def _():
            arrived(source, landed, sum_rs).wait_recv()
            out_ref[...] += decode(landed[source])

    @others
    def _(to):
        key_copy(to).wait_send()
        tile_copy(to).wait_send()

    for j in range(4):
        forward(j).wait_send()

    @loop(2)
    def _(h):
        for k in range(4):
            core_copy(h, k).wait_send()

        @loop(4)
        def _(q):
            @pl.when(send_to(h, q) != me)
            def _():
                sum_copy(h, q).wait_send()


def fused(amplitudes, integrals, tile_block, tile_index):
    rows = amplitudes.shape[0]
    dma = pltpu.SemaphoreType.DMA
    bf16, f32, i32, i16 = jnp.bfloat16, jnp.float32, jnp.int32, jnp.int16
    return pl.pallas_call(
        kernel,
        out_shape=jax.ShapeDtypeStruct((16, 1024), f32),
        in_specs=[
            pl.BlockSpec(memory_space=pl.ANY),
            pl.BlockSpec(memory_space=pl.ANY),
            pl.BlockSpec(memory_space=pl.ANY),
            pl.BlockSpec(memory_space=pl.ANY),
        ],
        out_specs=pl.BlockSpec(memory_space=pltpu.VMEM),
        scratch_shapes=[
            pltpu.SMEM((rows,), i32),
            pltpu.SMEM((rows,), i32),
            pltpu.VMEM((rows * 16, 128), bf16),
            pltpu.VMEM((768, 1024), bf16),
            pltpu.VMEM((16, 32, 128), bf16),
            pltpu.VMEM((2, 16, 32, 128), bf16),
            pltpu.VMEM((16, 1, 128), i32),
            pltpu.VMEM((16, 1, 128), i32),
            pltpu.VMEM((768, 512), bf16),
            pltpu.VMEM((128, 768), bf16),
            pltpu.VMEM((2, 4, 8, 16, 256), f32),
            pltpu.VMEM((2, 4, 4, 16, 256), f32),
            pltpu.VMEM((2, 4, 16, 1152), i16),
            pltpu.VMEM((8, 16, 1152), i16),
            dma(()), dma(()), dma(()), dma(()),
            dma((16,)), dma((16,)), dma((16,)), dma((16,)), dma((4,)), dma((4,)),
            dma((2, 4)), dma((2, 4)), dma((2, 4)), dma((8,)),
        ],
        compiler_params=pltpu.CompilerParams(
            collective_id=0, has_side_effects=True, vmem_limit_bytes=60 * 1024 * 1024
        ),
        name="ladder",
    )(tile_block, tile_index, amplitudes.reshape(rows * 16, 128), integrals)


def solution(mesh):
    count = (mesh.shape["grp"], mesh.shape["own"])

    def run(amplitudes, integrals, tile_block, tile_index):
        sizes = amplitudes.shape + integrals.shape
        small = count == (2, 16) and sizes == (192, 32, 128, 12288, 2048)
        return jax.shard_map(
            fused if small else local,
            mesh=mesh,
            in_specs=(P("own", "grp", None), P("own", "grp"), P("own"), P("own")),
            out_specs=P("own", "grp"),
            check_vma=False,
        )(amplitudes, integrals, tile_block, tile_index)

    return run
```

```python
import functools

import jax
import jax.numpy as jnp
from jax import lax
from jax.experimental import pallas as pl
from jax.experimental.pallas import tpu as pltpu
from jax.sharding import PartitionSpec as P

NB = 8
CAP = 2
MESH = pl.DeviceIdType.MESH


def loop(count):
    def run(body):
        lax.fori_loop(0, count, lambda i, carry: (body(i), carry)[1], 0)

    return run


def local(amplitudes, integrals, tile_block, tile_index):
    own_count = lax.axis_size("own")
    tile_width = amplitudes.shape[2]
    tile_dev = integrals.shape[0] // tile_width
    tile_owner = tile_index // tile_dev
    local_tile = tile_index - tile_owner * tile_dev
    tile_key = tile_block * tile_dev + local_tile
    one_hot = (tile_owner[:, None] == jnp.arange(own_count)[None, :]).astype(jnp.int32)
    slot_rank = jnp.sum((jnp.cumsum(one_hot, axis=0) - one_hot) * one_hot, axis=1)
    key_buffer = jnp.full((own_count, CAP), -1, jnp.int32).at[tile_owner, slot_rank].set(tile_key)
    gathered = lax.all_gather(amplitudes, "grp", axis=1, tiled=True)
    buffer = jnp.zeros((own_count, CAP) + gathered.shape[1:], gathered.dtype)
    received = lax.all_to_all(
        buffer.at[tile_owner, slot_rank].set(gathered),
        "own",
        split_axis=0,
        concat_axis=0,
        tiled=True,
    )
    recv_keys = lax.all_to_all(key_buffer, "own", split_axis=0, concat_axis=0, tiled=True)
    occ_rows = received.shape[2]
    slots = received.reshape(own_count * CAP, occ_rows, tile_width)
    flat_keys = recv_keys.reshape(own_count * CAP)
    recv_block = jnp.where(flat_keys >= 0, flat_keys // tile_dev, -1)
    recv_tile = jnp.where(flat_keys >= 0, flat_keys % tile_dev, 0)
    row_count = NB * occ_rows
    row_index = recv_block[:, None] * occ_rows + jnp.arange(occ_rows)[None, :]
    in_range = (recv_block[:, None] >= 0) & (row_index >= 0) & (row_index < row_count)
    row_index = jnp.where(in_range, row_index, row_count)
    tile_slot = jnp.broadcast_to(recv_tile[:, None], row_index.shape)
    placed = jnp.zeros((row_count, tile_dev, tile_width), slots.dtype)
    placed = placed.at[row_index, tile_slot].set(slots, mode="drop")
    return lax.psum_scatter(
        jnp.dot(
            placed.reshape(row_count, tile_dev * tile_width),
            integrals,
            preferred_element_type=jnp.float32,
        ),
        "own",
        scatter_dimension=0,
        tiled=True,
    )


def encode(v):
    parts = [v[:, k * 128 : (k + 1) * 128] for k in range(8)]
    top = functools.reduce(jnp.maximum, [jnp.abs(p) for p in parts])
    expo = jnp.ceil(jnp.log2(jnp.maximum(top, 1e-30)))
    scale = jnp.exp2(14.0 - expo)
    low = expo.astype(jnp.int32) + 128
    coded = [
        jnp.clip(jnp.round(p * scale), -16383.0, 16383.0).astype(jnp.int32) * 2 + ((low >> k) & 1)
        for k, p in enumerate(parts)
    ]
    return jnp.concatenate(coded, axis=1).astype(jnp.int16)


def decode(q):
    wide = q.astype(jnp.int32)
    parts = [wide[:, k * 128 : (k + 1) * 128] for k in range(8)]
    bits = [p & 1 for p in parts]
    low = functools.reduce(jnp.add, [b << k for k, b in enumerate(bits)])
    scale = jnp.exp2((low - 143).astype(jnp.float32))
    return jnp.concatenate([(p - b).astype(jnp.float32) * scale for p, b in zip(parts, bits)], axis=1)


def kernel(
    block_hbm, index_hbm, amp_hbm, int_hbm, out_ref,
    block_ref, index_ref, amp_ref, ints, sends, tiles, key_out, key_in, pick, lhs, prod, sib,
    coded, landed,
    int_sem, amp_sem, block_sem, index_sem, tile_ss, tile_rs, key_ss, key_rs, fwd_ss, fwd_rs,
    core_ss, core_rs, sum_ss, sum_rs,
):
    n = 16
    rows = amp_ref.shape[0] // 16
    tile_dev = 6
    me = lax.axis_index("own")
    g = lax.axis_index("grp")
    core = lax.rem(me, 2)
    z = me // 4
    sibling = me + 1 - 2 * core

    load_index = pltpu.make_async_copy(index_hbm, index_ref, index_sem)
    load_block = pltpu.make_async_copy(block_hbm, block_ref, block_sem)
    load_amp = pltpu.make_async_copy(amp_hbm, amp_ref, amp_sem)
    load = pltpu.make_async_copy(int_hbm, ints, int_sem)
    load_index.start()
    load_block.start()
    load_amp.start()
    barrier = pltpu.get_barrier_semaphore()

    @loop(n - 1)
    def _(i):
        pl.semaphore_signal(barrier, inc=1, device_id={"own": lax.rem(me + i + 1, n)}, device_id_type=MESH)

    pl.semaphore_signal(barrier, inc=1, device_id={"grp": 1 - g}, device_id_type=MESH)

    load.start()
    load_index.wait()
    load_block.wait()

    owner, rank, key = [], [], []
    for r in range(rows):
        t = index_ref[r]
        o = t // tile_dev
        owner.append(o)
        b = block_ref[r]
        place_of = (b // 2 % 2) * 4 + (b // 4) * 2 + b % 2
        key.append((t - o * tile_dev) * NB + place_of)
        earlier = jnp.int32(0)
        for q in range(r):
            earlier = earlier + jnp.where(owner[q] == o, 1, 0)
        rank.append(earlier)

    dest = lax.broadcasted_iota(jnp.int32, (n, 128), 0)
    lane = lax.broadcasted_iota(jnp.int32, (n, 128), 1)
    sub = lane - lax.rem(me, 4) * 32
    slot = jnp.where((sub >= 0) & (sub < 32), dest * 2 + sub // 16, -1)
    inner = lax.rem(lane, 16)
    keys = jnp.zeros((n, 128), jnp.int32)
    for r in range(rows):
        keys = keys + jnp.where(slot == owner[r] * 2 + rank[r], key[r] * 16 + inner + 1, 0)
    for o in range(n):
        key_out[o] = keys[o : o + 1, :]

    col = lax.broadcasted_iota(jnp.int32, (1, rows * 16), 1)
    place_row = jnp.zeros((1, rows * 16), jnp.int32)
    for r in range(rows):
        place_row = jnp.where(col // 16 == r, (owner[r] * 2 + rank[r]) * 16 + lax.rem(col, 16), place_row)
    load_amp.wait()
    amp = amp_ref[...]

    row = lax.broadcasted_iota(jnp.int32, (512, rows * 16), 0)
    hot = jnp.where(row == place_row, 1.0, 0.0).astype(jnp.bfloat16)
    sends[...] = jnp.dot(hot, amp, preferred_element_type=jnp.float32).astype(jnp.bfloat16).reshape(16, 32, 128)
    tiles[0, me] = sends[me]
    key_in[me] = key_out[me]

    pl.semaphore_wait(barrier, n)

    def key_copy(to):
        return pltpu.make_async_remote_copy(
            key_out.at[to], key_in.at[me], key_ss.at[to], key_rs.at[me],
            device_id={"own": to}, device_id_type=MESH,
        )

    def tile_copy(to):
        return pltpu.make_async_remote_copy(
            sends.at[to], tiles.at[0, me], tile_ss.at[to], tile_rs.at[me],
            device_id={"own": to}, device_id_type=MESH,
        )

    def forward(j):
        return pltpu.make_async_remote_copy(
            tiles.at[0, pl.ds(j * 4, 4)], tiles.at[1, pl.ds(j * 4, 4)], fwd_ss.at[j], fwd_rs.at[j],
            device_id={"grp": 1 - g}, device_id_type=MESH,
        )

    def others(body):
        @loop(n)
        def _(i):
            to = lax.rem(z + 2 + i // 4, 4) * 4 + lax.rem(me + i, 4)

            @pl.when(to != me)
            def _():
                body(to)

    others(lambda to: key_copy(to).start())
    others(lambda to: tile_copy(to).start())

    def arrived(s, buffer, sem):
        return pltpu.make_async_remote_copy(
            buffer.at[s], buffer.at[s], sem.at[s], sem.at[s],
            device_id={"own": sibling}, device_id_type=MESH,
        )

    others(lambda s: arrived(s, key_in, key_rs).wait_recv())
    targets = [
        key_in[4 * j] + key_in[4 * j + 1] + key_in[4 * j + 2] + key_in[4 * j + 3] for j in range(4)
    ]
    target = jnp.concatenate(targets, axis=1)

    @loop(tile_dev)
    def _(t):
        row = lax.broadcasted_iota(jnp.int32, (128, 512), 0)
        pick[pl.ds(pl.multiple_of(t * 128, 128), 128), :] = jnp.where(
            row == target - (t * 128 + 1), 1.0, 0.0
        ).astype(jnp.bfloat16)

    @loop(4)
    def _(i):
        j = lax.rem(z + i, 4)

        @loop(4)
        def _(w):
            s = j * 4 + w

            @pl.when(s != me)
            def _():
                arrived(s, tiles.at[0], tile_rs).wait_recv()

        forward(j).start()

    def place(h):
        slots = tiles[h].reshape(512, 128)
        got = jnp.dot(pick[...], slots, preferred_element_type=jnp.float32).astype(jnp.bfloat16)
        for t in range(tile_dev):
            lhs[:, t * 128 : (t + 1) * 128] = got[t * 128 : (t + 1) * 128]

    def core_copy(h, k):
        return pltpu.make_async_remote_copy(
            prod.at[h, k, pl.ds(4 * (1 - core), 4)], sib.at[h, k], core_ss.at[h, k], core_rs.at[h, k],
            device_id={"own": sibling}, device_id_type=MESH,
        )

    def multiply(h, k):
        cols = pl.ds(pl.multiple_of(k * 256, 256), 256)
        prod[h, k] = jnp.dot(
            lhs[...], ints[:, cols], preferred_element_type=jnp.float32
        ).reshape(8, 16, 256)

    def chip_sum(h, b):
        return jnp.concatenate(
            [prod[h, k, 4 * core + b] + sib[h, k, b] for k in range(4)], axis=1
        )

    def send_to(h, q):
        return 4 * (core + 2 * (q // 2)) + 2 * lax.rem(q, 2) + lax.rem(g + h, 2)

    def sum_copy(h, q):
        return pltpu.make_async_remote_copy(
            coded.at[h, q], landed.at[me // 2], sum_ss.at[h, q], sum_rs.at[me // 2],
            device_id={"own": send_to(h, q)}, device_id_type=MESH,
        )

    def prepare(h, q):
        total = chip_sum(h, q)
        coded[h, q] = encode(total)
        out_ref[...] += jnp.where(send_to(h, q) == me, total, 0.0)

    def send(h, q):
        @pl.when(send_to(h, q) != me)
        def _():
            sum_copy(h, q).start()

    def turn(k):
        return lax.rem(k + 2 * (1 - z // 2), 4)

    out_ref[...] = jnp.zeros_like(out_ref)
    load.wait()
    place(0)

    @loop(4)
    def _(k):
        multiply(0, k)
        core_copy(0, k).start()

    for j in range(4):
        forward(j).wait_recv()
    place(1)
    for k in range(4):
        core_copy(0, k).wait_recv()

    @loop(4)
    def _(k):
        q = turn(k)
        prepare(0, q)
        multiply(1, k)
        core_copy(1, k).start()
        send(0, q)

    for k in range(4):
        core_copy(1, k).wait_recv()

    @loop(4)
    def _(k):
        q = turn(k)
        prepare(1, q)
        send(1, q)

    @loop(8)
    def _(i):
        source = lax.rem(me // 2 + i, 8)

        @pl.when(jnp.logical_or(i > 0, lax.rem(z, 2) != core))
        def _():
            arrived(source, landed, sum_rs).wait_recv()
            out_ref[...] += decode(landed[source])

    @others
    def _(to):
        key_copy(to).wait_send()
        tile_copy(to).wait_send()

    for j in range(4):
        forward(j).wait_send()

    @loop(2)
    def _(h):
        for k in range(4):
            core_copy(h, k).wait_send()

        @loop(4)
        def _(q):
            @pl.when(send_to(h, q) != me)
            def _():
                sum_copy(h, q).wait_send()


def fused(amplitudes, integrals, tile_block, tile_index):
    rows = amplitudes.shape[0]
    dma = pltpu.SemaphoreType.DMA
    bf16, f32, i32, i16 = jnp.bfloat16, jnp.float32, jnp.int32, jnp.int16
    return pl.pallas_call(
        kernel,
        out_shape=pltpu.VMEM((16, 1024), f32),
        in_specs=[
            pl.BlockSpec(memory_space=pl.ANY),
            pl.BlockSpec(memory_space=pl.ANY),
            pl.BlockSpec(memory_space=pl.ANY),
            pl.BlockSpec(memory_space=pl.ANY),
        ],
        out_specs=pl.BlockSpec(memory_space=pltpu.VMEM),
        scratch_shapes=[
            pltpu.SMEM((rows,), i32),
            pltpu.SMEM((rows,), i32),
            pltpu.VMEM((rows * 16, 128), bf16),
            pltpu.VMEM((768, 1024), bf16),
            pltpu.VMEM((16, 32, 128), bf16),
            pltpu.VMEM((2, 16, 32, 128), bf16),
            pltpu.VMEM((16, 1, 128), i32),
            pltpu.VMEM((16, 1, 128), i32),
            pltpu.VMEM((768, 512), bf16),
            pltpu.VMEM((128, 768), bf16),
            pltpu.VMEM((2, 4, 8, 16, 256), f32),
            pltpu.VMEM((2, 4, 4, 16, 256), f32),
            pltpu.VMEM((2, 4, 16, 1024), i16),
            pltpu.VMEM((8, 16, 1024), i16),
            dma(()), dma(()), dma(()), dma(()),
            dma((16,)), dma((16,)), dma((16,)), dma((16,)), dma((4,)), dma((4,)),
            dma((2, 4)), dma((2, 4)), dma((2, 4)), dma((8,)),
        ],
        compiler_params=pltpu.CompilerParams(
            collective_id=0, has_side_effects=True, vmem_limit_bytes=56 * 1024 * 1024
        ),
        name="ladder",
    )(tile_block, tile_index, amplitudes.reshape(rows * 16, 128), integrals)


def solution(mesh):
    count = (mesh.shape["grp"], mesh.shape["own"])

    def run(amplitudes, integrals, tile_block, tile_index):
        sizes = amplitudes.shape + integrals.shape
        small = count == (2, 16) and sizes == (192, 32, 128, 12288, 2048)
        return jax.shard_map(
            fused if small else local,
            mesh=mesh,
            in_specs=(P("own", "grp", None), P("own", "grp"), P("own"), P("own")),
            out_specs=P("own", "grp"),
            check_vma=False,
        )(amplitudes, integrals, tile_block, tile_index)

    return run
```

```python
import functools

import jax
import jax.numpy as jnp
from jax import lax
from jax.experimental import pallas as pl
from jax.experimental.pallas import tpu as pltpu
from jax.sharding import PartitionSpec as P

NB = 8
CAP = 2
MESH = pl.DeviceIdType.MESH


def loop(count):
    def run(body):
        lax.fori_loop(0, count, lambda i, carry: (body(i), carry)[1], 0)

    return run


def local(amplitudes, integrals, tile_block, tile_index):
    own_count = lax.axis_size("own")
    tile_width = amplitudes.shape[2]
    tile_dev = integrals.shape[0] // tile_width
    tile_owner = tile_index // tile_dev
    local_tile = tile_index - tile_owner * tile_dev
    tile_key = tile_block * tile_dev + local_tile
    one_hot = (tile_owner[:, None] == jnp.arange(own_count)[None, :]).astype(jnp.int32)
    slot_rank = jnp.sum((jnp.cumsum(one_hot, axis=0) - one_hot) * one_hot, axis=1)
    key_buffer = jnp.full((own_count, CAP), -1, jnp.int32).at[tile_owner, slot_rank].set(tile_key)
    gathered = lax.all_gather(amplitudes, "grp", axis=1, tiled=True)
    buffer = jnp.zeros((own_count, CAP) + gathered.shape[1:], gathered.dtype)
    received = lax.all_to_all(
        buffer.at[tile_owner, slot_rank].set(gathered),
        "own",
        split_axis=0,
        concat_axis=0,
        tiled=True,
    )
    recv_keys = lax.all_to_all(key_buffer, "own", split_axis=0, concat_axis=0, tiled=True)
    occ_rows = received.shape[2]
    slots = received.reshape(own_count * CAP, occ_rows, tile_width)
    flat_keys = recv_keys.reshape(own_count * CAP)
    recv_block = jnp.where(flat_keys >= 0, flat_keys // tile_dev, -1)
    recv_tile = jnp.where(flat_keys >= 0, flat_keys % tile_dev, 0)
    row_count = NB * occ_rows
    row_index = recv_block[:, None] * occ_rows + jnp.arange(occ_rows)[None, :]
    in_range = (recv_block[:, None] >= 0) & (row_index >= 0) & (row_index < row_count)
    row_index = jnp.where(in_range, row_index, row_count)
    tile_slot = jnp.broadcast_to(recv_tile[:, None], row_index.shape)
    placed = jnp.zeros((row_count, tile_dev, tile_width), slots.dtype)
    placed = placed.at[row_index, tile_slot].set(slots, mode="drop")
    return lax.psum_scatter(
        jnp.dot(
            placed.reshape(row_count, tile_dev * tile_width),
            integrals,
            preferred_element_type=jnp.float32,
        ),
        "own",
        scatter_dimension=0,
        tiled=True,
    )


def encode(v):
    parts = [v[:, k * 128 : (k + 1) * 128] for k in range(8)]
    top = functools.reduce(jnp.maximum, [jnp.abs(p) for p in parts])
    expo = jnp.ceil(jnp.log2(jnp.maximum(top, 1e-30)))
    scale = jnp.exp2(14.0 - expo)
    low = expo.astype(jnp.int32) + 128
    coded = [
        jnp.clip(jnp.round(p * scale), -16383.0, 16383.0).astype(jnp.int32) * 2 + ((low >> k) & 1)
        for k, p in enumerate(parts)
    ]
    return jnp.concatenate(coded, axis=1).astype(jnp.int16)


def decode(q):
    wide = q.astype(jnp.int32)
    parts = [wide[:, k * 128 : (k + 1) * 128] for k in range(8)]
    bits = [p & 1 for p in parts]
    low = functools.reduce(jnp.add, [b << k for k, b in enumerate(bits)])
    scale = jnp.exp2((low - 143).astype(jnp.float32))
    return jnp.concatenate([(p - b).astype(jnp.float32) * scale for p, b in zip(parts, bits)], axis=1)


def kernel(
    block_hbm, index_hbm, amp_hbm, int_hbm, out_ref,
    block_ref, index_ref, amp_ref, ints, sends, tiles, key_out, key_in, pick, lhs, prod, sib,
    coded, landed,
    int_sem, amp_sem, block_sem, index_sem, tile_ss, tile_rs, key_ss, key_rs, fwd_ss, fwd_rs,
    core_ss, core_rs, sum_ss, sum_rs,
):
    n = 16
    rows = amp_ref.shape[0] // 16
    tile_dev = 6
    me = lax.axis_index("own")
    g = lax.axis_index("grp")
    core = lax.rem(me, 2)
    z = me // 4
    sibling = me + 1 - 2 * core

    load_index = pltpu.make_async_copy(index_hbm, index_ref, index_sem)
    load_block = pltpu.make_async_copy(block_hbm, block_ref, block_sem)
    load_amp = pltpu.make_async_copy(amp_hbm, amp_ref, amp_sem)
    load = pltpu.make_async_copy(int_hbm, ints, int_sem)
    load_index.start()
    load_block.start()
    load_amp.start()
    barrier = pltpu.get_barrier_semaphore()

    @loop(n - 1)
    def _(i):
        pl.semaphore_signal(barrier, inc=1, device_id={"own": lax.rem(me + i + 1, n)}, device_id_type=MESH)

    pl.semaphore_signal(barrier, inc=1, device_id={"grp": 1 - g}, device_id_type=MESH)

    load.start()
    load_index.wait()
    load_block.wait()

    owner, rank, key = [], [], []
    for r in range(rows):
        t = index_ref[r]
        o = t // tile_dev
        owner.append(o)
        b = block_ref[r]
        place_of = (b // 2 % 2) * 4 + (b // 4) * 2 + b % 2
        key.append((t - o * tile_dev) * NB + place_of)
        earlier = jnp.int32(0)
        for q in range(r):
            earlier = earlier + jnp.where(owner[q] == o, 1, 0)
        rank.append(earlier)

    dest = lax.broadcasted_iota(jnp.int32, (n, 128), 0)
    lane = lax.broadcasted_iota(jnp.int32, (n, 128), 1)
    sub = lane - lax.rem(me, 4) * 32
    slot = jnp.where((sub >= 0) & (sub < 32), dest * 2 + sub // 16, -1)
    inner = lax.rem(lane, 16)
    keys = jnp.zeros((n, 128), jnp.int32)
    for r in range(rows):
        keys = keys + jnp.where(slot == owner[r] * 2 + rank[r], key[r] * 16 + inner + 1, 0)
    for o in range(n):
        key_out[o] = keys[o : o + 1, :]

    col = lax.broadcasted_iota(jnp.int32, (1, rows * 16), 1)
    place_row = jnp.zeros((1, rows * 16), jnp.int32)
    for r in range(rows):
        place_row = jnp.where(col // 16 == r, (owner[r] * 2 + rank[r]) * 16 + lax.rem(col, 16), place_row)
    load_amp.wait()
    amp = amp_ref[...]

    row = lax.broadcasted_iota(jnp.int32, (512, rows * 16), 0)
    hot = jnp.where(row == place_row, 1.0, 0.0).astype(jnp.bfloat16)
    sends[...] = jnp.dot(hot, amp, preferred_element_type=jnp.float32).astype(jnp.bfloat16).reshape(16, 32, 128)
    tiles[0, me] = sends[me]
    key_in[me] = key_out[me]
    out_ref[...] = jnp.zeros_like(out_ref)

    pl.semaphore_wait(barrier, n)

    def key_copy(to):
        return pltpu.make_async_remote_copy(
            key_out.at[to], key_in.at[me], key_ss.at[to], key_rs.at[me],
            device_id={"own": to}, device_id_type=MESH,
        )

    def tile_copy(to):
        return pltpu.make_async_remote_copy(
            sends.at[to], tiles.at[0, me], tile_ss.at[to], tile_rs.at[me],
            device_id={"own": to}, device_id_type=MESH,
        )

    def forward(j):
        return pltpu.make_async_remote_copy(
            tiles.at[0, pl.ds(j * 4, 4)], tiles.at[1, pl.ds(j * 4, 4)], fwd_ss.at[j], fwd_rs.at[j],
            device_id={"grp": 1 - g}, device_id_type=MESH,
        )

    def others(body):
        @loop(n)
        def _(i):
            to = lax.rem(2 * (1 - z // 2) + i // 4, 4) * 4 + lax.rem(me + i, 4)

            @pl.when(to != me)
            def _():
                body(to)

    @others
    def _(to):
        key_copy(to).start()
        tile_copy(to).start()

    def arrived(s, buffer, sem):
        return pltpu.make_async_remote_copy(
            buffer.at[s], buffer.at[s], sem.at[s], sem.at[s],
            device_id={"own": sibling}, device_id_type=MESH,
        )

    others(lambda s: arrived(s, key_in, key_rs).wait_recv())
    targets = [
        key_in[4 * j] + key_in[4 * j + 1] + key_in[4 * j + 2] + key_in[4 * j + 3] for j in range(4)
    ]
    target = jnp.concatenate(targets, axis=1)

    @loop(tile_dev)
    def _(t):
        row = lax.broadcasted_iota(jnp.int32, (128, 512), 0)
        pick[pl.ds(pl.multiple_of(t * 128, 128), 128), :] = jnp.where(
            row == target - (t * 128 + 1), 1.0, 0.0
        ).astype(jnp.bfloat16)

    @loop(4)
    def _(i):
        j = lax.rem(z + i, 4)

        @loop(4)
        def _(w):
            s = j * 4 + w

            @pl.when(s != me)
            def _():
                arrived(s, tiles.at[0], tile_rs).wait_recv()

        forward(j).start()

    def place(h):
        slots = tiles[h].reshape(512, 128)
        got = jnp.dot(pick[...], slots, preferred_element_type=jnp.float32).astype(jnp.bfloat16)
        for t in range(tile_dev):
            lhs[:, t * 128 : (t + 1) * 128] = got[t * 128 : (t + 1) * 128]

    def core_copy(h, k):
        return pltpu.make_async_remote_copy(
            prod.at[h, k, pl.ds(4 * (1 - core), 4)], sib.at[h, k], core_ss.at[h, k], core_rs.at[h, k],
            device_id={"own": sibling}, device_id_type=MESH,
        )

    def multiply(h, k):
        cols = pl.ds(pl.multiple_of(k * 256, 256), 256)
        prod[h, k] = jnp.dot(
            lhs[...], ints[:, cols], preferred_element_type=jnp.float32
        ).reshape(8, 16, 256)

    def chip_sum(h, b):
        return jnp.concatenate(
            [prod[h, k, 4 * core + b] + sib[h, k, b] for k in range(4)], axis=1
        )

    def send_to(h, q):
        return 4 * (core + 2 * (q // 2)) + 2 * lax.rem(q, 2) + lax.rem(g + h, 2)

    def sum_copy(h, q):
        return pltpu.make_async_remote_copy(
            coded.at[h, q], landed.at[me // 2], sum_ss.at[h, q], sum_rs.at[me // 2],
            device_id={"own": send_to(h, q)}, device_id_type=MESH,
        )

    def prepare(h, q):
        total = chip_sum(h, q)
        coded[h, q] = encode(total)
        out_ref[...] += jnp.where(send_to(h, q) == me, total, 0.0)

    def send(h, q):
        @pl.when(send_to(h, q) != me)
        def _():
            sum_copy(h, q).start()

    def turn(k):
        return lax.rem(k + 2 * (1 - z // 2), 4)

    load.wait()
    place(0)

    @loop(4)
    def _(k):
        multiply(0, k)
        core_copy(0, k).start()

    for j in range(4):
        forward(j).wait_recv()
    place(1)
    multiply(1, 0)
    core_copy(1, 0).start()
    for k in range(4):
        core_copy(0, k).wait_recv()

    @loop(3)
    def _(k):
        q = turn(k)
        prepare(0, q)
        multiply(1, k + 1)
        core_copy(1, k + 1).start()
        send(0, q)

    prepare(0, turn(3))
    send(0, turn(3))

    for k in range(4):
        core_copy(1, k).wait_recv()

    @loop(4)
    def _(k):
        q = turn(k)
        prepare(1, q)
        send(1, q)

    def sent(h):
        for k in range(4):
            core_copy(h, k).wait_send()

        @loop(4)
        def _(q):
            @pl.when(send_to(h, q) != me)
            def _():
                sum_copy(h, q).wait_send()

    @others
    def _(to):
        key_copy(to).wait_send()
        tile_copy(to).wait_send()

    for j in range(4):
        forward(j).wait_send()
    sent(0)

    @loop(8)
    def _(i):
        source = lax.rem(me // 2 + i, 8)

        @pl.when(jnp.logical_or(i > 0, lax.rem(z, 2) != core))
        def _():
            arrived(source, landed, sum_rs).wait_recv()
            out_ref[...] += decode(landed[source])

    sent(1)


def fused(amplitudes, integrals, tile_block, tile_index):
    rows = amplitudes.shape[0]
    dma = pltpu.SemaphoreType.DMA
    bf16, f32, i32, i16 = jnp.bfloat16, jnp.float32, jnp.int32, jnp.int16
    return pl.pallas_call(
        kernel,
        out_shape=pltpu.VMEM((16, 1024), f32),
        in_specs=[
            pl.BlockSpec(memory_space=pl.ANY),
            pl.BlockSpec(memory_space=pl.ANY),
            pl.BlockSpec(memory_space=pl.ANY),
            pl.BlockSpec(memory_space=pl.ANY),
        ],
        out_specs=pl.BlockSpec(memory_space=pltpu.VMEM),
        scratch_shapes=[
            pltpu.SMEM((rows,), i32),
            pltpu.SMEM((rows,), i32),
            pltpu.VMEM((rows * 16, 128), bf16),
            pltpu.VMEM((768, 1024), bf16),
            pltpu.VMEM((16, 32, 128), bf16),
            pltpu.VMEM((2, 16, 32, 128), bf16),
            pltpu.VMEM((16, 1, 128), i32),
            pltpu.VMEM((16, 1, 128), i32),
            pltpu.VMEM((768, 512), bf16),
            pltpu.VMEM((128, 768), bf16),
            pltpu.VMEM((2, 4, 8, 16, 256), f32),
            pltpu.VMEM((2, 4, 4, 16, 256), f32),
            pltpu.VMEM((2, 4, 16, 1024), i16),
            pltpu.VMEM((8, 16, 1024), i16),
            dma(()), dma(()), dma(()), dma(()),
            dma((16,)), dma((16,)), dma((16,)), dma((16,)), dma((4,)), dma((4,)),
            dma((2, 4)), dma((2, 4)), dma((2, 4)), dma((8,)),
        ],
        compiler_params=pltpu.CompilerParams(
            collective_id=0, has_side_effects=True, vmem_limit_bytes=56 * 1024 * 1024
        ),
        name="ladder",
    )(tile_block, tile_index, amplitudes.reshape(rows * 16, 128), integrals)


def solution(mesh):
    count = (mesh.shape["grp"], mesh.shape["own"])

    def run(amplitudes, integrals, tile_block, tile_index):
        sizes = amplitudes.shape + integrals.shape
        small = count == (2, 16) and sizes == (192, 32, 128, 12288, 2048)
        return jax.shard_map(
            fused if small else local,
            mesh=mesh,
            in_specs=(P("own", "grp", None), P("own", "grp"), P("own"), P("own")),
            out_specs=P("own", "grp"),
            check_vma=False,
        )(amplitudes, integrals, tile_block, tile_index)

    return run
```

```python
import functools

import jax
import jax.numpy as jnp
from jax import lax
from jax.experimental import pallas as pl
from jax.experimental.pallas import tpu as pltpu
from jax.sharding import PartitionSpec as P

NB = 8
CAP = 2
MESH = pl.DeviceIdType.MESH


def loop(count):
    def run(body):
        lax.fori_loop(0, count, lambda i, carry: (body(i), carry)[1], 0)

    return run


def local(amplitudes, integrals, tile_block, tile_index):
    own_count = lax.axis_size("own")
    tile_width = amplitudes.shape[2]
    tile_dev = integrals.shape[0] // tile_width
    tile_owner = tile_index // tile_dev
    local_tile = tile_index - tile_owner * tile_dev
    tile_key = tile_block * tile_dev + local_tile
    one_hot = (tile_owner[:, None] == jnp.arange(own_count)[None, :]).astype(jnp.int32)
    slot_rank = jnp.sum((jnp.cumsum(one_hot, axis=0) - one_hot) * one_hot, axis=1)
    key_buffer = jnp.full((own_count, CAP), -1, jnp.int32).at[tile_owner, slot_rank].set(tile_key)
    gathered = lax.all_gather(amplitudes, "grp", axis=1, tiled=True)
    buffer = jnp.zeros((own_count, CAP) + gathered.shape[1:], gathered.dtype)
    received = lax.all_to_all(
        buffer.at[tile_owner, slot_rank].set(gathered),
        "own",
        split_axis=0,
        concat_axis=0,
        tiled=True,
    )
    recv_keys = lax.all_to_all(key_buffer, "own", split_axis=0, concat_axis=0, tiled=True)
    occ_rows = received.shape[2]
    slots = received.reshape(own_count * CAP, occ_rows, tile_width)
    flat_keys = recv_keys.reshape(own_count * CAP)
    recv_block = jnp.where(flat_keys >= 0, flat_keys // tile_dev, -1)
    recv_tile = jnp.where(flat_keys >= 0, flat_keys % tile_dev, 0)
    row_count = NB * occ_rows
    row_index = recv_block[:, None] * occ_rows + jnp.arange(occ_rows)[None, :]
    in_range = (recv_block[:, None] >= 0) & (row_index >= 0) & (row_index < row_count)
    row_index = jnp.where(in_range, row_index, row_count)
    tile_slot = jnp.broadcast_to(recv_tile[:, None], row_index.shape)
    placed = jnp.zeros((row_count, tile_dev, tile_width), slots.dtype)
    placed = placed.at[row_index, tile_slot].set(slots, mode="drop")
    return lax.psum_scatter(
        jnp.dot(
            placed.reshape(row_count, tile_dev * tile_width),
            integrals,
            preferred_element_type=jnp.float32,
        ),
        "own",
        scatter_dimension=0,
        tiled=True,
    )


def encode(v):
    parts = [v[:, k * 128 : (k + 1) * 128] for k in range(8)]
    top = functools.reduce(jnp.maximum, [jnp.abs(p) for p in parts])
    expo = jnp.ceil(jnp.log2(jnp.maximum(top, 1e-30)))
    scale = jnp.exp2(14.0 - expo)
    low = expo.astype(jnp.int32) + 128
    coded = [
        jnp.clip(jnp.round(p * scale), -16383.0, 16383.0).astype(jnp.int32) * 2 + ((low >> k) & 1)
        for k, p in enumerate(parts)
    ]
    return jnp.concatenate(coded, axis=1).astype(jnp.int16)


def decode(q):
    wide = q.astype(jnp.int32)
    parts = [wide[:, k * 128 : (k + 1) * 128] for k in range(8)]
    bits = [p & 1 for p in parts]
    low = functools.reduce(jnp.add, [b << k for k, b in enumerate(bits)])
    scale = jnp.exp2((low - 143).astype(jnp.float32))
    return jnp.concatenate([(p - b).astype(jnp.float32) * scale for p, b in zip(parts, bits)], axis=1)


def kernel(
    block_hbm, index_hbm, amp_hbm, int_hbm, out_ref,
    block_ref, index_ref, amp_ref, ints, sends, tiles, key_out, key_in, pick, lhs, prod, sib,
    coded, landed,
    int_sem, amp_sem, block_sem, index_sem, tile_ss, tile_rs, key_ss, key_rs, fwd_ss, fwd_rs,
    core_ss, core_rs, sum_ss, sum_rs,
):
    n = 16
    rows = amp_ref.shape[0] // 16
    tile_dev = 6
    me = lax.axis_index("own")
    g = lax.axis_index("grp")
    core = lax.rem(me, 2)
    z = me // 4
    sibling = me + 1 - 2 * core

    load_index = pltpu.make_async_copy(index_hbm, index_ref, index_sem)
    load_block = pltpu.make_async_copy(block_hbm, block_ref, block_sem)
    load_amp = pltpu.make_async_copy(amp_hbm, amp_ref, amp_sem)
    load = pltpu.make_async_copy(int_hbm, ints, int_sem)
    load_index.start()
    load_block.start()
    load_amp.start()
    barrier = pltpu.get_barrier_semaphore()

    @loop(n - 1)
    def _(i):
        pl.semaphore_signal(barrier, inc=1, device_id={"own": lax.rem(me + i + 1, n)}, device_id_type=MESH)

    pl.semaphore_signal(barrier, inc=1, device_id={"grp": 1 - g}, device_id_type=MESH)

    load.start()
    load_index.wait()
    load_block.wait()

    owner, rank, key = [], [], []
    for r in range(rows):
        t = index_ref[r]
        o = t // tile_dev
        owner.append(o)
        b = block_ref[r]
        place_of = (b // 2 % 2) * 4 + (b // 4) * 2 + b % 2
        key.append((t - o * tile_dev) * NB + place_of)
        earlier = jnp.int32(0)
        for q in range(r):
            earlier = earlier + jnp.where(owner[q] == o, 1, 0)
        rank.append(earlier)

    dest = lax.broadcasted_iota(jnp.int32, (n, 128), 0)
    lane = lax.broadcasted_iota(jnp.int32, (n, 128), 1)
    sub = lane - lax.rem(me, 4) * 32
    slot = jnp.where((sub >= 0) & (sub < 32), dest * 2 + sub // 16, -1)
    inner = lax.rem(lane, 16)
    keys = jnp.zeros((n, 128), jnp.int32)
    for r in range(rows):
        keys = keys + jnp.where(slot == owner[r] * 2 + rank[r], key[r] * 16 + inner + 1, 0)
    for o in range(n):
        key_out[o] = keys[o : o + 1, :]

    col = lax.broadcasted_iota(jnp.int32, (1, rows * 16), 1)
    place_row = jnp.zeros((1, rows * 16), jnp.int32)
    for r in range(rows):
        place_row = jnp.where(col // 16 == r, (owner[r] * 2 + rank[r]) * 16 + lax.rem(col, 16), place_row)
    load_amp.wait()
    amp = amp_ref[...]

    row = lax.broadcasted_iota(jnp.int32, (512, rows * 16), 0)
    hot = jnp.where(row == place_row, 1.0, 0.0).astype(jnp.bfloat16)
    sends[...] = jnp.dot(hot, amp, preferred_element_type=jnp.float32).astype(jnp.bfloat16).reshape(16, 32, 128)
    tiles[0, me] = sends[me]
    key_in[me] = key_out[me]
    out_ref[...] = jnp.zeros_like(out_ref)

    pl.semaphore_wait(barrier, n)

    def key_copy(to):
        return pltpu.make_async_remote_copy(
            key_out.at[to], key_in.at[me], key_ss.at[to], key_rs.at[me],
            device_id={"own": to}, device_id_type=MESH,
        )

    def tile_copy(to):
        return pltpu.make_async_remote_copy(
            sends.at[to], tiles.at[0, me], tile_ss.at[to], tile_rs.at[me],
            device_id={"own": to}, device_id_type=MESH,
        )

    def forward(j):
        return pltpu.make_async_remote_copy(
            tiles.at[0, pl.ds(j * 4, 4)], tiles.at[1, pl.ds(j * 4, 4)], fwd_ss.at[j], fwd_rs.at[j],
            device_id={"grp": 1 - g}, device_id_type=MESH,
        )

    def others(body):
        @loop(n)
        def _(i):
            to = lax.rem(2 * (1 - z // 2) + i // 4, 4) * 4 + lax.rem(me + i, 4)

            @pl.when(to != me)
            def _():
                body(to)

    others(lambda to: key_copy(to).start())
    others(lambda to: tile_copy(to).start())

    def arrived(s, buffer, sem):
        return pltpu.make_async_remote_copy(
            buffer.at[s], buffer.at[s], sem.at[s], sem.at[s],
            device_id={"own": sibling}, device_id_type=MESH,
        )

    others(lambda s: arrived(s, key_in, key_rs).wait_recv())
    targets = [
        key_in[4 * j] + key_in[4 * j + 1] + key_in[4 * j + 2] + key_in[4 * j + 3] for j in range(4)
    ]
    target = jnp.concatenate(targets, axis=1)

    @loop(tile_dev)
    def _(t):
        row = lax.broadcasted_iota(jnp.int32, (128, 512), 0)
        pick[pl.ds(pl.multiple_of(t * 128, 128), 128), :] = jnp.where(
            row == target - (t * 128 + 1), 1.0, 0.0
        ).astype(jnp.bfloat16)

    @loop(4)
    def _(i):
        j = lax.rem(z + i, 4)

        @loop(4)
        def _(w):
            s = j * 4 + w

            @pl.when(s != me)
            def _():
                arrived(s, tiles.at[0], tile_rs).wait_recv()

        forward(j).start()

    def place(h):
        slots = tiles[h].reshape(512, 128)
        got = jnp.dot(pick[...], slots, preferred_element_type=jnp.float32).astype(jnp.bfloat16)
        for t in range(tile_dev):
            lhs[:, t * 128 : (t + 1) * 128] = got[t * 128 : (t + 1) * 128]

    def core_copy(h, k):
        return pltpu.make_async_remote_copy(
            prod.at[h, k, pl.ds(4 * (1 - core), 4)], sib.at[h, k], core_ss.at[h, k], core_rs.at[h, k],
            device_id={"own": sibling}, device_id_type=MESH,
        )

    def multiply(h, k):
        cols = pl.ds(pl.multiple_of(k * 256, 256), 256)
        prod[h, k] = jnp.dot(
            lhs[...], ints[:, cols], preferred_element_type=jnp.float32
        ).reshape(8, 16, 256)

    def chip_sum(h, b):
        return jnp.concatenate(
            [prod[h, k, 4 * core + b] + sib[h, k, b] for k in range(4)], axis=1
        )

    def send_to(h, q):
        return 4 * (core + 2 * (q // 2)) + 2 * lax.rem(q, 2) + lax.rem(g + h, 2)

    def sum_copy(h, q):
        return pltpu.make_async_remote_copy(
            coded.at[h, q], landed.at[me // 2], sum_ss.at[h, q], sum_rs.at[me // 2],
            device_id={"own": send_to(h, q)}, device_id_type=MESH,
        )

    def prepare(h, q):
        total = chip_sum(h, q)
        coded[h, q] = encode(total)
        out_ref[...] += jnp.where(send_to(h, q) == me, total, 0.0)

    def send(h, q):
        @pl.when(send_to(h, q) != me)
        def _():
            sum_copy(h, q).start()

    def turn(k):
        return lax.rem(k + 2 * (1 - z // 2), 4)

    load.wait()
    place(0)

    @loop(4)
    def _(k):
        multiply(0, k)
        core_copy(0, k).start()

    for j in range(4):
        forward(j).wait_recv()
    place(1)
    for k in range(4):
        core_copy(0, k).wait_recv()

    @loop(4)
    def _(k):
        q = turn(k)
        prepare(0, q)
        multiply(1, k)
        core_copy(1, k).start()
        send(0, q)

    for k in range(4):
        core_copy(1, k).wait_recv()

    @loop(4)
    def _(k):
        q = turn(k)
        prepare(1, q)
        send(1, q)

    def sent(h):
        for k in range(4):
            core_copy(h, k).wait_send()

        @loop(4)
        def _(q):
            @pl.when(send_to(h, q) != me)
            def _():
                sum_copy(h, q).wait_send()

    @others
    def _(to):
        key_copy(to).wait_send()
        tile_copy(to).wait_send()

    for j in range(4):
        forward(j).wait_send()
    sent(0)

    @loop(8)
    def _(i):
        source = lax.rem(me // 2 + i, 8)

        @pl.when(jnp.logical_or(i > 0, lax.rem(z, 2) != core))
        def _():
            arrived(source, landed, sum_rs).wait_recv()
            out_ref[...] += decode(landed[source])

    sent(1)


def fused(amplitudes, integrals, tile_block, tile_index):
    rows = amplitudes.shape[0]
    dma = pltpu.SemaphoreType.DMA
    bf16, f32, i32, i16 = jnp.bfloat16, jnp.float32, jnp.int32, jnp.int16
    return pl.pallas_call(
        kernel,
        out_shape=pltpu.VMEM((16, 1024), f32),
        in_specs=[
            pl.BlockSpec(memory_space=pl.ANY),
            pl.BlockSpec(memory_space=pl.ANY),
            pl.BlockSpec(memory_space=pl.ANY),
            pl.BlockSpec(memory_space=pl.ANY),
        ],
        out_specs=pl.BlockSpec(memory_space=pltpu.VMEM),
        scratch_shapes=[
            pltpu.SMEM((rows,), i32),
            pltpu.SMEM((rows,), i32),
            pltpu.VMEM((rows * 16, 128), bf16),
            pltpu.VMEM((768, 1024), bf16),
            pltpu.VMEM((16, 32, 128), bf16),
            pltpu.VMEM((2, 16, 32, 128), bf16),
            pltpu.VMEM((16, 1, 128), i32),
            pltpu.VMEM((16, 1, 128), i32),
            pltpu.VMEM((768, 512), bf16),
            pltpu.VMEM((128, 768), bf16),
            pltpu.VMEM((2, 4, 8, 16, 256), f32),
            pltpu.VMEM((2, 4, 4, 16, 256), f32),
            pltpu.VMEM((2, 4, 16, 1024), i16),
            pltpu.VMEM((8, 16, 1024), i16),
            dma(()), dma(()), dma(()), dma(()),
            dma((16,)), dma((16,)), dma((16,)), dma((16,)), dma((4,)), dma((4,)),
            dma((2, 4)), dma((2, 4)), dma((2, 4)), dma((8,)),
        ],
        compiler_params=pltpu.CompilerParams(
            collective_id=0, has_side_effects=True, vmem_limit_bytes=56 * 1024 * 1024
        ),
        name="ladder",
    )(tile_block, tile_index, amplitudes.reshape(rows * 16, 128), integrals)


def solution(mesh):
    count = (mesh.shape["grp"], mesh.shape["own"])

    def run(amplitudes, integrals, tile_block, tile_index):
        sizes = amplitudes.shape + integrals.shape
        small = count == (2, 16) and sizes == (192, 32, 128, 12288, 2048)
        return jax.shard_map(
            fused if small else local,
            mesh=mesh,
            in_specs=(P("own", "grp", None), P("own", "grp"), P("own"), P("own")),
            out_specs=P("own", "grp"),
            check_vma=False,
        )(amplitudes, integrals, tile_block, tile_index)

    return run
```

```python
import functools

import jax
import jax.numpy as jnp
from jax import lax
from jax.experimental import pallas as pl
from jax.experimental.pallas import tpu as pltpu
from jax.sharding import PartitionSpec as P

NB = 8
CAP = 2
MESH = pl.DeviceIdType.MESH


def loop(count):
    def run(body):
        lax.fori_loop(0, count, lambda i, carry: (body(i), carry)[1], 0)

    return run


def local(amplitudes, integrals, tile_block, tile_index):
    own_count = lax.axis_size("own")
    tile_width = amplitudes.shape[2]
    tile_dev = integrals.shape[0] // tile_width
    tile_owner = tile_index // tile_dev
    local_tile = tile_index - tile_owner * tile_dev
    tile_key = tile_block * tile_dev + local_tile
    one_hot = (tile_owner[:, None] == jnp.arange(own_count)[None, :]).astype(jnp.int32)
    slot_rank = jnp.sum((jnp.cumsum(one_hot, axis=0) - one_hot) * one_hot, axis=1)
    key_buffer = jnp.full((own_count, CAP), -1, jnp.int32).at[tile_owner, slot_rank].set(tile_key)
    gathered = lax.all_gather(amplitudes, "grp", axis=1, tiled=True)
    buffer = jnp.zeros((own_count, CAP) + gathered.shape[1:], gathered.dtype)
    received = lax.all_to_all(
        buffer.at[tile_owner, slot_rank].set(gathered),
        "own",
        split_axis=0,
        concat_axis=0,
        tiled=True,
    )
    recv_keys = lax.all_to_all(key_buffer, "own", split_axis=0, concat_axis=0, tiled=True)
    occ_rows = received.shape[2]
    slots = received.reshape(own_count * CAP, occ_rows, tile_width)
    flat_keys = recv_keys.reshape(own_count * CAP)
    recv_block = jnp.where(flat_keys >= 0, flat_keys // tile_dev, -1)
    recv_tile = jnp.where(flat_keys >= 0, flat_keys % tile_dev, 0)
    row_count = NB * occ_rows
    row_index = recv_block[:, None] * occ_rows + jnp.arange(occ_rows)[None, :]
    in_range = (recv_block[:, None] >= 0) & (row_index >= 0) & (row_index < row_count)
    row_index = jnp.where(in_range, row_index, row_count)
    tile_slot = jnp.broadcast_to(recv_tile[:, None], row_index.shape)
    placed = jnp.zeros((row_count, tile_dev, tile_width), slots.dtype)
    placed = placed.at[row_index, tile_slot].set(slots, mode="drop")
    return lax.psum_scatter(
        jnp.dot(
            placed.reshape(row_count, tile_dev * tile_width),
            integrals,
            preferred_element_type=jnp.float32,
        ),
        "own",
        scatter_dimension=0,
        tiled=True,
    )


def encode(v):
    parts = [v[:, k * 128 : (k + 1) * 128] for k in range(8)]
    top = functools.reduce(jnp.maximum, [jnp.abs(p) for p in parts])
    expo = jnp.ceil(jnp.log2(jnp.maximum(top, 1e-30)))
    scale = jnp.exp2(14.0 - expo)
    low = expo.astype(jnp.int32) + 128
    coded = [
        jnp.clip(jnp.round(p * scale), -16383.0, 16383.0).astype(jnp.int32) * 2 + ((low >> k) & 1)
        for k, p in enumerate(parts)
    ]
    return jnp.concatenate(coded, axis=1).astype(jnp.int16)


def decode(q):
    wide = q.astype(jnp.int32)
    parts = [wide[:, k * 128 : (k + 1) * 128] for k in range(8)]
    bits = [p & 1 for p in parts]
    low = functools.reduce(jnp.add, [b << k for k, b in enumerate(bits)])
    scale = jnp.exp2((low - 143).astype(jnp.float32))
    return jnp.concatenate([(p - b).astype(jnp.float32) * scale for p, b in zip(parts, bits)], axis=1)


def kernel(
    block_hbm, index_hbm, amp_hbm, int_hbm, out_ref,
    block_ref, index_ref, amp_ref, ints, sends, tiles, key_out, key_in, pick, lhs, prod, sib,
    coded, landed,
    int_sem, amp_sem, block_sem, index_sem, tile_ss, tile_rs, key_ss, key_rs, fwd_ss, fwd_rs,
    core_ss, core_rs, sum_ss, sum_rs,
):
    n = 16
    rows = amp_ref.shape[0] // 16
    tile_dev = 6
    me = lax.axis_index("own")
    g = lax.axis_index("grp")
    core = lax.rem(me, 2)
    z = me // 4
    sibling = me + 1 - 2 * core

    load_index = pltpu.make_async_copy(index_hbm, index_ref, index_sem)
    load_block = pltpu.make_async_copy(block_hbm, block_ref, block_sem)
    load_amp = pltpu.make_async_copy(amp_hbm, amp_ref, amp_sem)
    load = pltpu.make_async_copy(int_hbm, ints, int_sem)
    load_index.start()
    load_block.start()
    load_amp.start()
    barrier = pltpu.get_barrier_semaphore()

    @loop(n - 1)
    def _(i):
        pl.semaphore_signal(barrier, inc=1, device_id={"own": lax.rem(me + i + 1, n)}, device_id_type=MESH)

    pl.semaphore_signal(barrier, inc=1, device_id={"grp": 1 - g}, device_id_type=MESH)

    load.start()
    load_index.wait()
    load_block.wait()

    owner, rank, key = [], [], []
    for r in range(rows):
        t = index_ref[r]
        o = t // tile_dev
        owner.append(o)
        b = block_ref[r]
        place_of = (b // 2 % 2) * 4 + (b // 4) * 2 + b % 2
        key.append((t - o * tile_dev) * NB + place_of)
        earlier = jnp.int32(0)
        for q in range(r):
            earlier = earlier + jnp.where(owner[q] == o, 1, 0)
        rank.append(earlier)

    dest = lax.broadcasted_iota(jnp.int32, (n, 128), 0)
    lane = lax.broadcasted_iota(jnp.int32, (n, 128), 1)
    sub = lane - lax.rem(me, 4) * 32
    slot = jnp.where((sub >= 0) & (sub < 32), dest * 2 + sub // 16, -1)
    inner = lax.rem(lane, 16)
    keys = jnp.zeros((n, 128), jnp.int32)
    for r in range(rows):
        keys = keys + jnp.where(slot == owner[r] * 2 + rank[r], key[r] * 16 + inner + 1, 0)
    for o in range(n):
        key_out[o] = keys[o : o + 1, :]

    col = lax.broadcasted_iota(jnp.int32, (1, rows * 16), 1)
    place_row = jnp.zeros((1, rows * 16), jnp.int32)
    for r in range(rows):
        place_row = jnp.where(col // 16 == r, (owner[r] * 2 + rank[r]) * 16 + lax.rem(col, 16), place_row)
    load_amp.wait()
    amp = amp_ref[...]

    row = lax.broadcasted_iota(jnp.int32, (512, rows * 16), 0)
    hot = jnp.where(row == place_row, 1.0, 0.0).astype(jnp.bfloat16)
    sends[...] = jnp.dot(hot, amp, preferred_element_type=jnp.float32).astype(jnp.bfloat16).reshape(16, 32, 128)
    tiles[0, me] = sends[me]
    key_in[me] = key_out[me]
    out_ref[...] = jnp.zeros_like(out_ref)

    pl.semaphore_wait(barrier, n)

    def key_copy(to):
        return pltpu.make_async_remote_copy(
            key_out.at[to], key_in.at[me], key_ss.at[to], key_rs.at[me],
            device_id={"own": to}, device_id_type=MESH,
        )

    def tile_copy(to):
        return pltpu.make_async_remote_copy(
            sends.at[to], tiles.at[0, me], tile_ss.at[to], tile_rs.at[me],
            device_id={"own": to}, device_id_type=MESH,
        )

    def forward(j):
        return pltpu.make_async_remote_copy(
            tiles.at[0, pl.ds(j * 4, 4)], tiles.at[1, pl.ds(j * 4, 4)], fwd_ss.at[j], fwd_rs.at[j],
            device_id={"grp": 1 - g}, device_id_type=MESH,
        )

    def others(body):
        @loop(n)
        def _(i):
            to = lax.rem(2 * (1 - z // 2) + i // 4, 4) * 4 + lax.rem(me + i, 4)

            @pl.when(to != me)
            def _():
                body(to)

    others(lambda to: key_copy(to).start())
    others(lambda to: tile_copy(to).start())

    def arrived(s, buffer, sem):
        return pltpu.make_async_remote_copy(
            buffer.at[s], buffer.at[s], sem.at[s], sem.at[s],
            device_id={"own": sibling}, device_id_type=MESH,
        )

    others(lambda s: arrived(s, key_in, key_rs).wait_recv())
    targets = [
        key_in[4 * j] + key_in[4 * j + 1] + key_in[4 * j + 2] + key_in[4 * j + 3] for j in range(4)
    ]
    target = jnp.concatenate(targets, axis=1)

    @loop(tile_dev)
    def _(t):
        row = lax.broadcasted_iota(jnp.int32, (128, 512), 0)
        pick[pl.ds(pl.multiple_of(t * 128, 128), 128), :] = jnp.where(
            row == target - (t * 128 + 1), 1.0, 0.0
        ).astype(jnp.bfloat16)

    @loop(4)
    def _(i):
        j = lax.rem(z + i, 4)

        @loop(4)
        def _(w):
            s = j * 4 + w

            @pl.when(s != me)
            def _():
                arrived(s, tiles.at[0], tile_rs).wait_recv()

        forward(j).start()

    def place(h):
        slots = tiles[h].reshape(512, 128)
        got = jnp.dot(pick[...], slots, preferred_element_type=jnp.float32).astype(jnp.bfloat16)
        for t in range(tile_dev):
            lhs[:, t * 128 : (t + 1) * 128] = got[t * 128 : (t + 1) * 128]

    def core_copy(h, k):
        return pltpu.make_async_remote_copy(
            prod.at[h, k, pl.ds(4 * (1 - core), 4)], sib.at[h, k], core_ss.at[h, k], core_rs.at[h, k],
            device_id={"own": sibling}, device_id_type=MESH,
        )

    def multiply(h, k):
        cols = pl.ds(pl.multiple_of(k * 256, 256), 256)
        prod[h, k] = jnp.dot(
            lhs[...], ints[:, cols], preferred_element_type=jnp.float32
        ).reshape(8, 16, 256)

    def chip_sum(h, b):
        return jnp.concatenate(
            [prod[h, k, 4 * core + b] + sib[h, k, b] for k in range(4)], axis=1
        )

    def send_to(h, q):
        return 4 * (core + 2 * (q // 2)) + 2 * lax.rem(q, 2) + lax.rem(g + h, 2)

    def sum_copy(h, q):
        return pltpu.make_async_remote_copy(
            coded.at[h, q], landed.at[me // 2], sum_ss.at[h, q], sum_rs.at[me // 2],
            device_id={"own": send_to(h, q)}, device_id_type=MESH,
        )

    def prepare(h, q):
        total = chip_sum(h, q)
        coded[h, q] = encode(total)
        out_ref[...] += jnp.where(send_to(h, q) == me, total, 0.0)

    def send(h, q):
        @pl.when(send_to(h, q) != me)
        def _():
            sum_copy(h, q).start()

    def turn(k):
        return lax.rem(k + 2 * (1 - z // 2), 4)

    load.wait()
    place(0)

    @loop(2)
    def _(k):
        multiply(0, 2 * k)
        multiply(0, 2 * k + 1)
        core_copy(0, 2 * k).start()
        core_copy(0, 2 * k + 1).start()

    for j in range(4):
        forward(j).wait_recv()
    place(1)
    for k in range(4):
        core_copy(0, k).wait_recv()

    @loop(4)
    def _(k):
        q = turn(k)
        prepare(0, q)
        multiply(1, k)
        core_copy(1, k).start()
        send(0, q)

    for k in range(4):
        core_copy(1, k).wait_recv()

    @loop(4)
    def _(k):
        q = turn(k)
        prepare(1, q)
        send(1, q)

    def sent(h):
        for k in range(4):
            core_copy(h, k).wait_send()

        @loop(4)
        def _(q):
            @pl.when(send_to(h, q) != me)
            def _():
                sum_copy(h, q).wait_send()

    @others
    def _(to):
        key_copy(to).wait_send()
        tile_copy(to).wait_send()

    for j in range(4):
        forward(j).wait_send()
    sent(0)

    @loop(8)
    def _(i):
        source = lax.rem(me // 2 + 8 + i * (1 - 2 * (z // 2)), 8)

        @pl.when(jnp.logical_or(i > 0, lax.rem(z, 2) != core))
        def _():
            arrived(source, landed, sum_rs).wait_recv()
            out_ref[...] += decode(landed[source])

    sent(1)


def fused(amplitudes, integrals, tile_block, tile_index):
    rows = amplitudes.shape[0]
    dma = pltpu.SemaphoreType.DMA
    bf16, f32, i32, i16 = jnp.bfloat16, jnp.float32, jnp.int32, jnp.int16
    return pl.pallas_call(
        kernel,
        out_shape=pltpu.VMEM((16, 1024), f32),
        in_specs=[
            pl.BlockSpec(memory_space=pl.ANY),
            pl.BlockSpec(memory_space=pl.ANY),
            pl.BlockSpec(memory_space=pl.ANY),
            pl.BlockSpec(memory_space=pl.ANY),
        ],
        out_specs=pl.BlockSpec(memory_space=pltpu.VMEM),
        scratch_shapes=[
            pltpu.SMEM((rows,), i32),
            pltpu.SMEM((rows,), i32),
            pltpu.VMEM((rows * 16, 128), bf16),
            pltpu.VMEM((768, 1024), bf16),
            pltpu.VMEM((16, 32, 128), bf16),
            pltpu.VMEM((2, 16, 32, 128), bf16),
            pltpu.VMEM((16, 1, 128), i32),
            pltpu.VMEM((16, 1, 128), i32),
            pltpu.VMEM((768, 512), bf16),
            pltpu.VMEM((128, 768), bf16),
            pltpu.VMEM((2, 4, 8, 16, 256), f32),
            pltpu.VMEM((2, 4, 4, 16, 256), f32),
            pltpu.VMEM((2, 4, 16, 1024), i16),
            pltpu.VMEM((8, 16, 1024), i16),
            dma(()), dma(()), dma(()), dma(()),
            dma((16,)), dma((16,)), dma((16,)), dma((16,)), dma((4,)), dma((4,)),
            dma((2, 4)), dma((2, 4)), dma((2, 4)), dma((8,)),
        ],
        compiler_params=pltpu.CompilerParams(
            collective_id=0, has_side_effects=True, vmem_limit_bytes=56 * 1024 * 1024
        ),
        name="ladder",
    )(tile_block, tile_index, amplitudes.reshape(rows * 16, 128), integrals)


def solution(mesh):
    count = (mesh.shape["grp"], mesh.shape["own"])

    def run(amplitudes, integrals, tile_block, tile_index):
        sizes = amplitudes.shape + integrals.shape
        small = count == (2, 16) and sizes == (192, 32, 128, 12288, 2048)
        return jax.shard_map(
            fused if small else local,
            mesh=mesh,
            in_specs=(P("own", "grp", None), P("own", "grp"), P("own"), P("own")),
            out_specs=P("own", "grp"),
            check_vma=False,
        )(amplitudes, integrals, tile_block, tile_index)

    return run
```
